512 devices in a mesh: blk: 128 (over z_lo, y, x), freq: 4 (over z_hi, core).
Axes of the slice: x: 4, y: 4, z: 16 (z_hi: 2, z_lo: 8; z = z_hi * 8 + z_lo), core: 2. Of those that a mesh axis runs over, the one named last changes fastest.
Arguments:
- samples: bfloat16 [1024, 64, 2048], P('blk', 'freq'), may hold values from -6 to 6
- channel_lists: int32 [4, 128, 2], replicated, may hold values from 0 to 1023, as said below
- channel_counts: int32 [4, 128], P('freq', 'blk'), may hold values from 0 to 2, as said below
Outputs:
- visibilities: bfloat16 [4, 128, 2, 136, 2, 4096], P('freq', 'blk')
The draws below stay inside these ranges and needn't reach their ends.
Inputs may be any that keep to these rules, and one draw needn't show every extreme that they name: `channel_lists`: the slots of owner (f, b) hold channels of the f-th quarter, f * 256 to (f + 1) * 256 - 1, distinct within one owner; only the first channel_counts[f, b] slots are live. `channel_counts`: in every quarter some owner has all 2 slots live.
All inputs are finite; a program needn't handle non-finite values.
Results may differ from the reference program's by a relative error of at most 0.0078.
Values may be sent and summed in bfloat16 or wider, within the bound.
No kernel may reach another device: no remote copies, remote signals or barrier semaphores. Data moves between devices by JAX's collectives and lax.ppermute only.
A program may use at most 128 MiB of HBM per device.

```python
import math
import jax
import jax.numpy as jnp
import numpy as np
from jax import lax

INPUTS = 1024
FRAME = 2048
TAPS = 16
SPECTRA = 64
QUARTER = 256
CAP = 2
N_BLK = 128
N_FREQ = 4


def draw_channel_lists(key, part):
    quarter_keys = jax.random.split(jax.random.fold_in(key, 11), N_FREQ)
    positions = jnp.arange(N_BLK * CAP, dtype=jnp.int32) % QUARTER
    quarters = []
    for quarter_idx in range(N_FREQ):
        shuffled = jax.random.permutation(quarter_keys[quarter_idx], QUARTER).astype(jnp.int32)
        quarters.append(shuffled[positions] + quarter_idx * QUARTER)
    return jnp.stack(quarters).reshape(N_FREQ, N_BLK, CAP).astype(jnp.int32)


def draw_channel_counts(key, part):
    base_counts = jax.random.randint(jax.random.fold_in(key, 13), (N_FREQ, N_BLK), 0, CAP + 1)
    full_owner = jax.random.randint(jax.random.fold_in(key, 17), (N_FREQ, 1), 0, N_BLK)
    marked = jnp.arange(N_BLK, dtype=jnp.int32)[None, :] == full_owner
    return jnp.where(marked, CAP, base_counts).astype(jnp.int32)


def shard_levels(key, shape, pieces, smallest, largest):
    def one(axis_at, shards_of):
        heights = jax.random.uniform(jax.random.fold_in(jax.random.fold_in(key, 6), axis_at), (shards_of,), jnp.float32, smallest / len(pieces), largest / len(pieces))
        return jnp.repeat(jnp.exp(heights), shape[axis_at] // shards_of).reshape((-1,) + (1,) * (len(shape) - axis_at - 1))

    factor_of = one(*pieces[0])
    for cut in pieces[1:]:
        factor_of = factor_of * one(*cut)
    return factor_of


def gaussian(stream_key, dims, scale, most, pieces=(), held_as=jnp.bfloat16):
    gain = shard_levels(stream_key, dims, pieces, -0.22, 0.18) if pieces else 1.0
    array = jax.random.normal(stream_key, dims, jnp.float32) * scale * gain
    return jnp.minimum(jnp.maximum(array, -most), most).astype(held_as)


def setup_inputs(seed: int = 0) -> dict:
    arg_keys = jax.random.split(jax.random.key(seed), 4)
    samples = gaussian(arg_keys[0], (INPUTS, SPECTRA, FRAME), 1.0, 6.0, ((0, 128), (1, 4)))
    channel_lists = draw_channel_lists(jax.random.fold_in(arg_keys[3], 71), 0)
    channel_counts = draw_channel_counts(jax.random.fold_in(arg_keys[3], 71), 0)
    return dict(samples=samples, channel_lists=channel_lists, channel_counts=channel_counts)


def window_taps(frame_len, tap_count):
    total_len = frame_len * tap_count
    positions = jnp.arange(total_len, dtype=jnp.int32).astype(jnp.float32)
    centred = (positions - 0.5 * total_len + 0.5) / frame_len
    hann_part = 0.5 - 0.5 * jnp.cos(2.0 * math.pi / total_len * (positions + 0.5))
    shaped = jnp.sinc(centred) * hann_part
    shaped = shaped * lax.rsqrt(jnp.sum(shaped * shaped) / frame_len)
    return shaped.reshape(tap_count, frame_len)

def polyphase(extended, window_shape, spec_count):
    tap_count = window_shape.shape[0]
    accumulated = jnp.zeros((extended.shape[0], spec_count, extended.shape[2]), jnp.float32)
    for tap_index in range(tap_count):
        accumulated = accumulated + window_shape[tap_index] * extended[:, tap_index:tap_index + spec_count, :].astype(jnp.float32)
    return accumulated.astype(jnp.bfloat16)

def fourier_table(block_start, block_width, frame_len):
    channel_ids = block_start + jnp.arange(block_width, dtype=jnp.int32)
    sample_ids = jnp.arange(frame_len, dtype=jnp.int32)
    phase_index = channel_ids[:, None] * sample_ids[None, :] % frame_len
    angles = phase_index.astype(jnp.float32) * (2.0 * math.pi / frame_len)
    norm_scale = 1.0 / math.sqrt(frame_len)
    return jnp.stack([jnp.cos(angles) * norm_scale, -jnp.sin(angles) * norm_scale]).astype(jnp.bfloat16)

def channelize(filtered, channel_total):
    frame_len = filtered.shape[2]
    block_width = 128 if channel_total % 128 == 0 else channel_total
    starts = jnp.arange(channel_total // block_width, dtype=jnp.int32) * block_width
    filtered_wide = filtered.astype(jnp.float32)

    def one_block(block_start):
        table = fourier_table(block_start, block_width, frame_len).astype(jnp.float32)
        return jnp.einsum('rcn,isn->cirs', table, filtered_wide).astype(jnp.bfloat16)
    blocks = lax.map(one_block, starts)
    return blocks.reshape(channel_total, -1)

def correlate(slot_data, tile_count):
    slot_total = slot_data.shape[0]
    input_total = slot_data.shape[1]
    width = slot_data.shape[2]
    middle = width // 2
    turned = jnp.concatenate([-slot_data[..., middle:], slot_data[..., :middle]], axis=-1)
    tile_size = input_total // tile_count
    row_tiles, col_tiles = np.triu_indices(tile_count)
    tiled = slot_data.reshape(slot_total, tile_count, tile_size, width)
    tiled_turned = turned.reshape(slot_total, tile_count, tile_size, width)
    left_tiles = tiled[:, row_tiles]
    right_tiles = tiled[:, col_tiles]
    right_turned = tiled_turned[:, col_tiles]
    real_part = jnp.einsum('kpar,kpbr->kpab', left_tiles, right_tiles)
    imag_part = jnp.einsum('kpar,kpbr->kpab', left_tiles, right_turned)
    picked = jnp.stack([real_part, imag_part], axis=2) / middle
    return picked.reshape(slot_total, picked.shape[1], 2, tile_size * tile_size).astype(jnp.bfloat16)

def reference(samples, channel_lists, channel_counts):
    input_total = samples.shape[0]
    spec_total = samples.shape[1]
    tap_count = TAPS
    tile_count = max(1, input_total // 64)
    window_shape = window_taps(samples.shape[2], tap_count)
    extended = jnp.concatenate([samples[:, spec_total - (tap_count - 1):], samples], axis=1)
    filtered = polyphase(extended, window_shape, spec_total)
    channel_total = samples.shape[2] // 2
    spectra = channelize(filtered, channel_total).reshape(channel_total, input_total, 2 * spec_total)
    freq_total, owner_total, slot_cap = channel_lists.shape
    flat_lists = channel_lists.reshape(freq_total * owner_total, slot_cap)
    flat_counts = channel_counts.reshape(freq_total * owner_total)

    def one_owner(owner_args):
        slot_channels, owner_count = owner_args
        slot_data = jnp.take(spectra, slot_channels, axis=0).astype(jnp.float32)
        tiles = correlate(slot_data, tile_count)
        live_slots = jnp.arange(slot_cap, dtype=jnp.int32) < owner_count
        return jnp.where(live_slots[:, None, None, None], tiles, jnp.zeros_like(tiles))
    results = lax.map(one_owner, (flat_lists, flat_counts))
    return results.reshape((freq_total, owner_total) + results.shape[1:])
```

```python
import math

import jax
import jax.numpy as jnp
import ml_dtypes
import numpy as np
from jax import lax
from jax.experimental import pallas as pl
from jax.experimental.pallas import tpu as pltpu
from jax.sharding import PartitionSpec as P

FRAME = 2048
HALF = 1024
TAPS = 16
INS = 8
OUT_T = 24
COLS = INS * OUT_T
LANES = 2 * COLS
QUARTER = 256
N_BLK = 128
N_FREQ = 4
TILES = 16
PAIRS = 136
GROUPS = ((0, 2), (0, 2), (0, 1, 2), (1,))


def window_taps():
    total_len = FRAME * TAPS
    m = np.arange(total_len, dtype=np.float64)
    shaped = np.sinc((m - total_len / 2 + 0.5) / FRAME)
    shaped = shaped * (0.5 - 0.5 * np.cos(2.0 * np.pi * (m + 0.5) / total_len))
    shaped = shaped / np.sqrt(np.sum(shaped * shaped) / FRAME)
    return shaped.reshape(TAPS, FRAME).astype(np.float32)


def fourier_halves():
    channels = np.arange(1024).reshape(4, 128, 2).transpose(0, 2, 1)
    phase = channels[..., None] * np.arange(HALF) % FRAME
    angle = phase * (2.0 * np.pi / FRAME)
    scale = 1.0 / math.sqrt(FRAME)
    both = np.concatenate([np.cos(angle) * scale, -np.sin(angle) * scale], axis=2)
    return both.astype(np.float32).astype(ml_dtypes.bfloat16)


def message_lane(r, col):
    if col < 128:
        return 256 * r + col
    return 128 + 64 * r + col - 128


def merge_matrices():
    blocks = []
    for pair, tiles in enumerate(GROUPS):
        block = np.zeros((N_FREQ, len(tiles), 128, 2, 128), np.float32)
        for f in range(N_FREQ):
            for h in range(2):
                for t in range(OUT_T):
                    local = OUT_T * (f % 2) + t
                    if local > 46:
                        continue
                    spectrum = (32 * (f // 2) + local) % 64
                    for r in range(2):
                        lane = message_lane(r, (2 * pair + h) * OUT_T + t)
                        block[f, tiles.index(lane // 128), lane % 128, h, r * 64 + spectrum] = 1.0
        blocks.append(block.reshape(-1, 256))
    return np.concatenate(blocks).astype(ml_dtypes.bfloat16)


def nt_dot(a, b):
    return lax.dot_general(a, b, (((1,), (1,)), ((), ())), preferred_element_type=jnp.float32)


def channel_kernel(core_ref, own_ref, other_ref, window_ref, table_ref, list_ref, out_ref, u_ref, v_ref):
    step = pl.program_id(0)

    @pl.when(step == 0)
    def _():
        second = core_ref[0] == 1
        width = 256
        u_ref[COLS:, :] = jnp.zeros((256 - COLS, HALF), jnp.bfloat16)
        v_ref[COLS:, :] = jnp.zeros((256 - COLS, HALF), jnp.bfloat16)

        def filtered(i, start):
            lanes = pl.ds(pl.multiple_of(start, width), width)
            own = own_ref[i, :, lanes].astype(jnp.float32)
            other = other_ref[i, :, lanes].astype(jnp.float32)
            zero = jnp.zeros((8, width), jnp.float32)
            extended = jnp.concatenate(
                [
                    jnp.where(second, other[8:], zero),
                    jnp.where(second, own[:8], zero),
                    jnp.where(second, own[8:], own[:8]),
                    jnp.where(second, zero, own[8:]),
                    jnp.where(second, zero, other[:8]),
                ],
                axis=0,
            )
            total = window_ref[7:8, lanes] * extended[8:32] + window_ref[15:16, lanes] * extended[16:40]
            for by in range(1, 8):
                moved = extended[by : by + 32]
                total = total + window_ref[by - 1 : by, lanes] * moved[0:24]
                total = total + window_ref[by + 7 : by + 8, lanes] * moved[8:32]
            return total

        def one(index, carry):
            pair = index // (HALF // width)
            start = (index % (HALF // width)) * width
            rows = pl.ds(pl.multiple_of(pair * 48, 16), 48)
            lanes = pl.ds(pl.multiple_of(start, width), width)
            low = [filtered(2 * pair + h, start) for h in range(2)]
            high = [filtered(2 * pair + h, start + HALF) for h in range(2)]
            low = jnp.concatenate(low, axis=0)
            high = jnp.concatenate(high, axis=0)
            u_ref[rows, lanes] = (low + high).astype(jnp.bfloat16)
            v_ref[rows, lanes] = (low - high).astype(jnp.bfloat16)
            return carry

        lax.fori_loop(0, (INS // 2) * (HALF // width), one, 0)

    halves = []
    for parity, folded in enumerate((u_ref, v_ref)):
        y = nt_dot(table_ref[0, parity], folded[...])
        middle = y[:128, 128:] + pltpu.roll(y[128:, 128:], 64, 1)
        halves.append(jnp.concatenate([y[:128, :128], middle, y[128:, :128]], axis=1))
    spectra = jnp.concatenate(halves, axis=0).astype(jnp.bfloat16)
    channels = list_ref[0]
    place = (channels & 1) * 128 + ((channels & 255) >> 1)
    picks = (lax.broadcasted_iota(jnp.int32, (QUARTER, QUARTER), 0) == place).astype(jnp.float32)
    out_ref[...] = jnp.dot(
        picks.T.astype(jnp.bfloat16), spectra, preferred_element_type=jnp.float32
    ).astype(jnp.bfloat16)


def channel_messages(core, own, other, lists):
    window = jnp.asarray(window_taps())
    table = jnp.asarray(fourier_halves())
    return pl.pallas_call(
        channel_kernel,
        grid=(N_FREQ,),
        in_specs=[
            pl.BlockSpec(memory_space=pltpu.SMEM),
            pl.BlockSpec((INS, 16, FRAME), lambda q: (0, 0, 0)),
            pl.BlockSpec((INS, 16, FRAME), lambda q: (0, 0, 0)),
            pl.BlockSpec((TAPS, FRAME), lambda q: (0, 0)),
            pl.BlockSpec((1, 2, 256, HALF), lambda q: (q, 0, 0, 0)),
            pl.BlockSpec((1, 1, QUARTER), lambda q: (q, 0, 0)),
        ],
        out_specs=pl.BlockSpec((QUARTER, LANES), lambda q: (q, 0)),
        out_shape=jax.ShapeDtypeStruct((N_FREQ * QUARTER, LANES), jnp.bfloat16),
        scratch_shapes=[pltpu.VMEM((256, HALF), jnp.bfloat16), pltpu.VMEM((256, HALF), jnp.bfloat16)],
        compiler_params=pltpu.CompilerParams(vmem_limit_bytes=40 << 20),
        name="channels",
    )(core, own, other, window, table, lists)


def correlate_kernel(count_ref, got_ref, merge_ref, out_ref, right_all, even_all, odd_all, left_ref, right_ref):
    slot = pl.program_id(0)

    @pl.when(slot == 0)
    def _():
        sign = jnp.where(lax.broadcasted_iota(jnp.int32, (1, 128), 1) < 64, 1.0, -1.0)
        base = 0
        for pair, tiles in enumerate(GROUPS):
            depth = N_FREQ * len(tiles) * 128
            parts = [
                got_ref[f * 256 : (f + 1) * 256, tile * 128 : (tile + 1) * 128]
                for f in range(N_FREQ)
                for tile in tiles
            ]
            both = jnp.dot(
                jnp.concatenate(parts, axis=1),
                merge_ref[base : base + depth, :],
                preferred_element_type=jnp.float32,
            )
            base += depth
            for h in range(2):
                plain = both[:, h * 128 : (h + 1) * 128]
                turned = pltpu.roll(plain, 64, 1) * sign
                right_all[pl.ds(2 * pair + h, 256, stride=8), :] = plain
                left_all = (even_all, odd_all)[h]
                left_all[pl.ds(2 * pair, 256, stride=8), :] = plain
                left_all[pl.ds(2 * pair + 1, 256, stride=8), :] = turned

    live = slot < count_ref[0, 0]

    @pl.when(live)
    def _():
        def tile_of(ref, tile):
            return jnp.concatenate(
                [
                    ref[pl.ds(pl.multiple_of((tile * 8 + b) * 16 + slot * 8, 8), 8), :]
                    for b in range(8)
                ],
                axis=0,
            ).astype(jnp.bfloat16)

        for tile in range(TILES):
            rows = slice(tile * 64, tile * 64 + 64)
            left_ref[rows, :128] = tile_of(even_all, tile)
            left_ref[rows, 128:] = tile_of(odd_all, tile)
            right_ref[rows, :] = tile_of(right_all, tile)
        zero = jnp.zeros((64, 128), jnp.bfloat16)
        for m in range(TILES // 2):
            rhs = []
            for q in (2 * m, 2 * m + 1):
                column = right_ref[q * 64 : (q + 1) * 64, :]
                rhs.append(jnp.concatenate([column, zero], axis=1))
                rhs.append(jnp.concatenate([zero, column], axis=1))
            products = nt_dot(left_ref[: (2 * m + 2) * 64, :], jnp.concatenate(rhs, axis=0))
            for h in range(2):
                q = 2 * m + h
                for p in range(q + 1):
                    t = TILES * p - p * (p - 1) // 2 + q - p
                    piece = products[p * 64 : (p + 1) * 64, h * 128 : (h + 1) * 128]
                    out_ref[0, t] = (piece * (1.0 / 64.0)).astype(jnp.bfloat16)

    @pl.when(jnp.logical_not(live))
    def _():
        out_ref[...] = jnp.zeros(out_ref.shape, out_ref.dtype)


def visibility_tiles(counts, got):
    merge = jnp.asarray(merge_matrices())
    return pl.pallas_call(
        correlate_kernel,
        grid=(2,),
        in_specs=[
            pl.BlockSpec(memory_space=pltpu.SMEM),
            pl.BlockSpec((1024, LANES), lambda j: (0, 0)),
            pl.BlockSpec(merge.shape, lambda j: (0, 0)),
        ],
        out_specs=pl.BlockSpec((1, PAIRS, 64, 128), lambda j: (j, 0, 0, 0)),
        out_shape=jax.ShapeDtypeStruct((2, PAIRS, 64, 128), jnp.bfloat16),
        scratch_shapes=[
            pltpu.VMEM((2048, 128), jnp.float32),
            pltpu.VMEM((2048, 128), jnp.float32),
            pltpu.VMEM((2048, 128), jnp.float32),
            pltpu.VMEM((1024, 256), jnp.bfloat16),
            pltpu.VMEM((1024, 128), jnp.bfloat16),
        ],
        compiler_params=pltpu.CompilerParams(vmem_limit_bytes=40 << 20),
        name="correlate",
    )(counts, got, merge)


def shards(samples, channel_lists, channel_counts):
    freq = lax.axis_index("freq")
    core = (freq % 2).astype(jnp.int32).reshape(1)
    other = lax.ppermute(samples, "freq", [(i, i ^ 1) for i in range(N_FREQ)])
    lists = channel_lists.reshape(N_FREQ, 1, QUARTER)
    messages = channel_messages(core, samples, other, lists)
    got = lax.all_to_all(
        messages.reshape(N_FREQ * N_BLK, 2, LANES), ("freq", "blk"), 0, 0, tiled=True
    ).reshape(1024, LANES)
    tiles = visibility_tiles(channel_counts, got)
    tiles = tiles.reshape(2, PAIRS, 32, 2, 128).transpose(0, 1, 3, 2, 4)
    return tiles.reshape(1, 1, 2, PAIRS, 2, 4096)


def solution(mesh):
    in_specs = (P("blk", "freq", None), P(), P("freq", "blk"))
    out_specs = P("freq", "blk", None, None, None, None)
    return jax.shard_map(shards, mesh=mesh, in_specs=in_specs, out_specs=out_specs, check_vma=False)
```

```python
import math

import jax
import jax.numpy as jnp
import ml_dtypes
import numpy as np
from jax import lax
from jax.experimental import pallas as pl
from jax.experimental.pallas import tpu as pltpu
from jax.sharding import Mesh, PartitionSpec as P

FRAME = 2048
HALF = 1024
TAPS = 16
INS = 8
OUT_T = 24
QUARTER = 256
N_BLK = 128
N_FREQ = 4
TILES = 16
PAIRS = 136
GROUPS = ((0, 1), (0, 1), (1, 2), (1, 2))


def window_taps():
    total_len = FRAME * TAPS
    m = np.arange(total_len, dtype=np.float64)
    shaped = np.sinc((m - total_len / 2 + 0.5) / FRAME)
    shaped = shaped * (0.5 - 0.5 * np.cos(2.0 * np.pi * (m + 0.5) / total_len))
    shaped = shaped / np.sqrt(np.sum(shaped * shaped) / FRAME)
    return shaped.reshape(TAPS, FRAME).astype(np.float32)


def fourier_halves():
    channels = np.arange(1024).reshape(4, 128, 2).transpose(0, 2, 1)
    phase = channels[..., None] * np.arange(HALF) % FRAME
    angle = phase * (2.0 * np.pi / FRAME)
    scale = 1.0 / math.sqrt(FRAME)
    both = np.concatenate([np.cos(angle) * scale, -np.sin(angle) * scale], axis=2)
    return both.astype(np.float32).astype(ml_dtypes.bfloat16)


def message_lane(core, i, t, r):
    if 16 * core <= 2 * t < 32 + 16 * core:
        return i // 4 * 256 + 64 * r + i % 4 * 16 + t - 8 * core
    return 128 + 64 * r + i * 8 + t % 8


def merge_matrices():
    blocks = []
    for pair, tiles in enumerate(GROUPS):
        block = np.zeros((N_FREQ, len(tiles), 128, 2, 128), np.float32)
        for f in range(N_FREQ):
            for h in range(2):
                for t in range(OUT_T):
                    local = OUT_T * (f % 2) + t
                    if local > 46:
                        continue
                    spectrum = (32 * (f // 2) + local) % 64
                    for r in range(2):
                        lane = message_lane(f % 2, 2 * pair + h, t, r)
                        block[f, tiles.index(lane // 128), lane % 128, h, r * 64 + spectrum] = 1.0
        blocks.append(block.reshape(-1, 256))
    return np.concatenate(blocks).astype(ml_dtypes.bfloat16)


def nt_dot(a, b):
    return lax.dot_general(a, b, (((1,), (1,)), ((), ())), preferred_element_type=jnp.float32)


def filtered(extended, window_ref, lanes):
    count = extended.shape[0] - 16
    total = window_ref[7:8, lanes] * extended[8 : 8 + count] + window_ref[15:16, lanes] * extended[16:]
    for by in range(1, 8):
        moved = extended[by : by + count + 8]
        total = total + window_ref[by - 1 : by, lanes] * moved[:count]
        total = total + window_ref[by + 7 : by + 8, lanes] * moved[8:]
    return total


def fold_into(u_ref, v_ref, row, group, width, extended_of, window_ref):
    def one(index, carry):
        first = index // (HALF // width) * group
        start = (index % (HALF // width)) * width
        parts = []
        for base in (0, HALF):
            lanes = pl.ds(pl.multiple_of(start + base, width), width)
            parts.append(
                jnp.concatenate(
                    [filtered(extended_of(first + h, lanes), window_ref, lanes) for h in range(group)],
                    axis=0,
                )
            )
        rows = pl.ds(pl.multiple_of(row + index // (HALF // width) * 16, 16), 16)
        lanes = pl.ds(pl.multiple_of(start, width), width)
        u_ref[rows, lanes] = (parts[0] + parts[1]).astype(jnp.bfloat16)
        v_ref[rows, lanes] = (parts[0] - parts[1]).astype(jnp.bfloat16)
        return carry

    lax.fori_loop(0, INS // group * (HALF // width), one, 0)


def own_kernel(core_ref, own_ref, window_ref, u_ref, v_ref):
    second = core_ref[0] == 1

    def extended_of(i, lanes):
        own = own_ref[i, :, lanes].astype(jnp.float32)
        zero = jnp.zeros_like(own)
        return jnp.concatenate([jnp.where(second, own, zero), jnp.where(second, zero, own)], axis=0)

    fold_into(u_ref, v_ref, 0, 1, 512, extended_of, window_ref)


def channel_kernel(
    core_ref, own_ref, other_ref, window_ref, table_any, list_ref, ua_ref, va_ref, out_ref, u_ref, v_ref, table_ref, rows_ref, sems
):
    step = pl.program_id(0)

    @pl.when(step == 0)
    def _():
        for q in range(N_FREQ):
            pltpu.make_async_copy(table_any.at[q], table_ref.at[q], sems.at[q]).start()
        second = core_ref[0] == 1

        def extended_of(i, lanes):
            own = own_ref[i, :, lanes].astype(jnp.float32)
            other = other_ref[i, :, lanes].astype(jnp.float32)
            return jnp.concatenate(
                [
                    jnp.where(second, other[8:], own[:8]),
                    jnp.where(second, own[:8], own[8:]),
                    jnp.where(second, own[8:], other[:8]),
                ],
                axis=0,
            )

        u_ref[:128, :] = ua_ref[...]
        v_ref[:128, :] = va_ref[...]
        u_ref[192:, :] = jnp.zeros((64, HALF), jnp.bfloat16)
        v_ref[192:, :] = jnp.zeros((64, HALF), jnp.bfloat16)
        fold_into(u_ref, v_ref, 128, 2, 512, extended_of, window_ref)

    pltpu.make_async_copy(table_any.at[step], table_ref.at[step], sems.at[step]).wait()
    low = lax.broadcasted_iota(jnp.int32, (1, 128), 1) < 64
    halves = []
    for parity, folded in enumerate((u_ref, v_ref)):
        y = nt_dot(table_ref[step, parity], folded[...])
        re, im = y[:128, :128], y[128:, :128]
        rest = y[:128, 128:] + pltpu.roll(y[128:, 128:], 64, 1)
        first = jnp.where(low, re, pltpu.roll(im, 64, 1))
        last = jnp.where(low, pltpu.roll(re, 64, 1), im)
        halves.append(jnp.concatenate([first, rest, last], axis=1))
    spectra = jnp.concatenate(halves, axis=0).astype(jnp.bfloat16)
    channels = list_ref[0]
    place = (channels & 1) * 128 + ((channels & 255) >> 1)
    picks = (lax.broadcasted_iota(jnp.int32, (QUARTER, QUARTER), 0) == place).astype(jnp.float32)
    picked = jnp.dot(picks.T.astype(jnp.bfloat16), spectra, preferred_element_type=jnp.float32)
    for tile in range(3):
        for slot in range(2):
            rows_ref[pl.ds(tile * 2 + slot, N_BLK, stride=6), :] = picked[
                slot * N_BLK : (slot + 1) * N_BLK, tile * 128 : (tile + 1) * 128
            ]
    out_ref[...] = rows_ref[...].astype(jnp.bfloat16)


def own_part(core, own, window):
    return pl.pallas_call(
        own_kernel,
        in_specs=[
            pl.BlockSpec(memory_space=pltpu.SMEM),
            pl.BlockSpec(memory_space=pltpu.VMEM),
            pl.BlockSpec(memory_space=pltpu.VMEM),
        ],
        out_specs=[pl.BlockSpec(memory_space=pltpu.VMEM)] * 2,
        out_shape=[jax.ShapeDtypeStruct((128, HALF), jnp.bfloat16)] * 2,
        compiler_params=pltpu.CompilerParams(vmem_limit_bytes=57 << 20),
        cost_estimate=pl.CostEstimate(flops=10_000_000, bytes_accessed=2_000_000, transcendentals=0),
        name="own",
    )(core, own, window)


def channel_messages(core, own, other, lists):
    window = jnp.asarray(window_taps())
    table = jnp.asarray(fourier_halves())
    ua, va = own_part(core, own, window)
    half = pl.BlockSpec((128, HALF), lambda q: (0, 0))
    return pl.pallas_call(
        channel_kernel,
        grid=(N_FREQ,),
        in_specs=[
            pl.BlockSpec(memory_space=pltpu.SMEM),
            pl.BlockSpec((INS, 16, FRAME), lambda q: (0, 0, 0)),
            pl.BlockSpec((INS, 16, FRAME), lambda q: (0, 0, 0)),
            pl.BlockSpec((TAPS, FRAME), lambda q: (0, 0)),
            pl.BlockSpec(memory_space=pltpu.HBM),
            pl.BlockSpec((1, 1, QUARTER), lambda q: (q, 0, 0)),
            half,
            half,
        ],
        out_specs=pl.BlockSpec((N_BLK * 6, 128), lambda q: (q % 2 * 2 + q // 2, 0)),
        out_shape=jax.ShapeDtypeStruct((N_FREQ * N_BLK * 6, 128), jnp.bfloat16),
        scratch_shapes=[
            pltpu.VMEM((256, HALF), jnp.bfloat16),
            pltpu.VMEM((256, HALF), jnp.bfloat16),
            pltpu.VMEM(table.shape, jnp.bfloat16),
            pltpu.VMEM((N_BLK * 6, 128), jnp.float32),
            pltpu.SemaphoreType.DMA((N_FREQ,)),
        ],
        compiler_params=pltpu.CompilerParams(vmem_limit_bytes=57 << 20),
        name="channels",
    )(core, own, other, window, table, lists, ua, va)


def correlate_kernel(count_ref, got_ref, merge_ref, out_ref, rows_ref, right_all, even_all, odd_all, left_ref, right_ref):
    slot = pl.program_id(0)

    @pl.when(slot == 0)
    def _():
        sign = jnp.where(lax.broadcasted_iota(jnp.int32, (1, 128), 1) < 64, 1.0, -1.0)
        rows_ref[...] = got_ref[...].astype(jnp.float32)
        sources = {}
        for f in range(N_FREQ):
            for tile in range(3):
                start = (f % 2 * 2 + f // 2) * N_BLK * 6 + tile * 2
                sources[f, tile] = jnp.concatenate(
                    [rows_ref[pl.ds(start + j, N_BLK, stride=6), :] for j in range(2)], axis=0
                ).astype(jnp.bfloat16)
        base = 0
        for pair, tiles in enumerate(GROUPS):
            depth = N_FREQ * len(tiles) * 128
            parts = [sources[f, tile] for f in range(N_FREQ) for tile in tiles]
            both = jnp.dot(
                jnp.concatenate(parts, axis=1),
                merge_ref[base : base + depth, :],
                preferred_element_type=jnp.float32,
            )
            base += depth
            for h in range(2):
                plain = both[:, h * 128 : (h + 1) * 128]
                turned = pltpu.roll(plain, 64, 1) * sign
                right_all[pl.ds(2 * pair + h, 256, stride=8), :] = plain
                left_all = (even_all, odd_all)[h]
                left_all[pl.ds(2 * pair, 256, stride=8), :] = plain
                left_all[pl.ds(2 * pair + 1, 256, stride=8), :] = turned

    live = slot < count_ref[0, 0]

    @pl.when(live)
    def _():
        def tile_of(ref, tile):
            pieces = []
            for b in range(tile * 8, tile * 8 + 8):
                place = b % 4 * 32 + b // 4 % 4 * 8 + b // 16
                pieces.append(ref[pl.ds(pl.multiple_of(slot * 1024 + place * 8, 8), 8), :])
            return jnp.concatenate(pieces, axis=0).astype(jnp.bfloat16)

        for tile in range(TILES):
            rows = slice(tile * 64, tile * 64 + 64)
            left_ref[rows, :128] = tile_of(even_all, tile)
            left_ref[rows, 128:] = tile_of(odd_all, tile)
            right_ref[rows, :] = tile_of(right_all, tile)
        zero = jnp.zeros((64, 128), jnp.bfloat16)
        for m in range(TILES // 2):
            rhs = []
            for q in (2 * m, 2 * m + 1):
                column = right_ref[q * 64 : (q + 1) * 64, :]
                rhs.append(jnp.concatenate([column, zero], axis=1))
                rhs.append(jnp.concatenate([zero, column], axis=1))
            products = nt_dot(left_ref[: (2 * m + 2) * 64, :], jnp.concatenate(rhs, axis=0))
            for h in range(2):
                q = 2 * m + h
                for p in range(q + 1):
                    t = TILES * p - p * (p - 1) // 2 + q - p
                    piece = products[p * 64 : (p + 1) * 64, h * 128 : (h + 1) * 128]
                    out_ref[0, t] = (piece * (1.0 / 64.0)).astype(jnp.bfloat16)

    @pl.when(jnp.logical_not(live))
    def _():
        out_ref[...] = jnp.zeros(out_ref.shape, out_ref.dtype)


def visibility_tiles(counts, got):
    merge = jnp.asarray(merge_matrices())
    return pl.pallas_call(
        correlate_kernel,
        grid=(2,),
        in_specs=[
            pl.BlockSpec(memory_space=pltpu.SMEM),
            pl.BlockSpec((N_FREQ * N_BLK * 6, 128), lambda j: (0, 0)),
            pl.BlockSpec(merge.shape, lambda j: (0, 0)),
        ],
        out_specs=pl.BlockSpec((1, PAIRS, 64, 128), lambda j: (j, 0, 0, 0)),
        out_shape=jax.ShapeDtypeStruct((2, PAIRS, 64, 128), jnp.bfloat16),
        scratch_shapes=[
            pltpu.VMEM((N_FREQ * N_BLK * 6, 128), jnp.float32),
            pltpu.VMEM((2048, 128), jnp.float32),
            pltpu.VMEM((2048, 128), jnp.float32),
            pltpu.VMEM((2048, 128), jnp.float32),
            pltpu.VMEM((1024, 256), jnp.bfloat16),
            pltpu.VMEM((1024, 128), jnp.bfloat16),
        ],
        compiler_params=pltpu.CompilerParams(vmem_limit_bytes=40 << 20),
        name="correlate",
    )(counts, got, merge)


def shards(samples, channel_lists, channel_counts):
    core = lax.axis_index("core").astype(jnp.int32).reshape(1)
    other = lax.ppermute(samples, "core", [(0, 1), (1, 0)])
    lists = channel_lists.reshape(N_FREQ, 8, 4, 4, 2).transpose(0, 4, 3, 2, 1).reshape(N_FREQ, 1, QUARTER)
    messages = channel_messages(core, samples, other, lists)
    got = lax.all_to_all(
        messages.reshape(N_FREQ * N_BLK, 3, 2, 128), ("core", "z_hi", "x", "y", "z_lo"), 0, 0, tiled=True
    ).reshape(N_FREQ * N_BLK * 6, 128)
    tiles = visibility_tiles(channel_counts, got)
    tiles = tiles.reshape(2, PAIRS, 32, 2, 128).transpose(0, 1, 3, 2, 4)
    return tiles.reshape(1, 1, 2, PAIRS, 2, 4096)


def solution(mesh):
    fine = Mesh(mesh.devices.reshape(8, 4, 4, 2, 2), ("z_lo", "y", "x", "z_hi", "core"))
    blk, freq = ("z_lo", "y", "x"), ("z_hi", "core")
    in_specs = (P(blk, freq, None), P(), P(freq, blk))
    out_specs = P(freq, blk, None, None, None, None)
    return jax.shard_map(shards, mesh=fine, in_specs=in_specs, out_specs=out_specs, check_vma=False)
```

```python
import math

import jax
import jax.numpy as jnp
import ml_dtypes
import numpy as np
from jax import lax
from jax.experimental import pallas as pl
from jax.experimental.pallas import tpu as pltpu
from jax.sharding import Mesh, PartitionSpec as P

FRAME = 2048
HALF = 1024
TAPS = 16
INS = 8
OUT_T = 24
QUARTER = 256
N_BLK = 128
N_FREQ = 4
TILES = 16
PAIRS = 136
GROUPS = ((0, 1), (0, 1), (1, 2), (1, 2))


def window_taps():
    total_len = FRAME * TAPS
    m = np.arange(total_len, dtype=np.float64)
    shaped = np.sinc((m - total_len / 2 + 0.5) / FRAME)
    shaped = shaped * (0.5 - 0.5 * np.cos(2.0 * np.pi * (m + 0.5) / total_len))
    shaped = shaped / np.sqrt(np.sum(shaped * shaped) / FRAME)
    return shaped.reshape(TAPS, FRAME).astype(np.float32)


def fourier_halves():
    channels = np.arange(1024).reshape(4, 128, 2).transpose(0, 2, 1)
    phase = channels[..., None] * np.arange(HALF) % FRAME
    angle = phase * (2.0 * np.pi / FRAME)
    scale = 1.0 / math.sqrt(FRAME)
    both = np.concatenate([np.cos(angle) * scale, -np.sin(angle) * scale], axis=2)
    return both.astype(np.float32).astype(ml_dtypes.bfloat16)


def message_lane(core, i, t, r):
    if 16 * core <= 2 * t < 32 + 16 * core:
        return i // 4 * 256 + 64 * r + i % 4 * 16 + t - 8 * core
    return 128 + 64 * r + i * 8 + t % 8


def merge_matrices():
    blocks = []
    for pair, tiles in enumerate(GROUPS):
        block = np.zeros((N_FREQ, len(tiles), 128, 2, 128), np.float32)
        for f in range(N_FREQ):
            for h in range(2):
                for t in range(OUT_T):
                    local = OUT_T * (f % 2) + t
                    if local > 46:
                        continue
                    spectrum = (32 * (f // 2) + local) % 64
                    for r in range(2):
                        lane = message_lane(f % 2, 2 * pair + h, t, r)
                        block[f, tiles.index(lane // 128), lane % 128, h, r * 64 + spectrum] = 1.0
        blocks.append(block.reshape(-1, 256))
    return np.concatenate(blocks).astype(ml_dtypes.bfloat16)


def nt_dot(a, b):
    return lax.dot_general(a, b, (((1,), (1,)), ((), ())), preferred_element_type=jnp.float32)


def filtered(extended, window_ref, lanes):
    count = extended.shape[0] - 16
    total = window_ref[7:8, lanes] * extended[8 : 8 + count] + window_ref[15:16, lanes] * extended[16:]
    for by in range(1, 8):
        moved = extended[by : by + count + 8]
        total = total + window_ref[by - 1 : by, lanes] * moved[:count]
        total = total + window_ref[by + 7 : by + 8, lanes] * moved[8:]
    return total


def fold_into(u_ref, v_ref, row, inputs, group, width, extended_of, window_ref):
    def one(index, carry):
        step = index // (HALF // width)
        start = (index % (HALF // width)) * width
        parts = []
        for base in (0, HALF):
            lanes = pl.ds(pl.multiple_of(start + base, width), width)
            parts.append(
                jnp.concatenate(
                    [
                        filtered(extended_of(inputs[0] + step * group + h, lanes), window_ref, lanes)
                        for h in range(group)
                    ],
                    axis=0,
                )
            )
        rows = pl.ds(pl.multiple_of(row + step * 16, 16), 16)
        lanes = pl.ds(pl.multiple_of(start, width), width)
        u_ref[rows, lanes] = (parts[0] + parts[1]).astype(jnp.bfloat16)
        v_ref[rows, lanes] = (parts[0] - parts[1]).astype(jnp.bfloat16)
        return carry

    lax.fori_loop(0, len(inputs) // group * (HALF // width), one, 0)


def own_kernel(core_ref, own_hbm, window_hbm, table_hbm, u_ref, v_ref, own_ref, window_ref, table_ref, sems):
    window_copy = pltpu.make_async_copy(window_hbm, window_ref, sems.at[0])
    table_copy = pltpu.make_async_copy(table_hbm, table_ref, sems.at[1])
    own_copies = [
        pltpu.make_async_copy(own_hbm.at[c : c + 2], own_ref.at[c : c + 2], sems.at[2 + c // 2])
        for c in range(0, INS, 2)
    ]
    for copy in [window_copy, *own_copies, table_copy]:
        copy.start()
    second = core_ref[0] == 1

    def extended_of(i, lanes):
        own = own_ref[i, :, lanes].astype(jnp.float32)
        zero = jnp.zeros_like(own)
        return jnp.concatenate([jnp.where(second, own, zero), jnp.where(second, zero, own)], axis=0)

    window_copy.wait()
    for c, copy in enumerate(own_copies):
        copy.wait()
        fold_into(u_ref, v_ref, c * 32, range(2 * c, 2 * c + 2), 1, 512, extended_of, window_ref)
    table_copy.wait()


def channel_kernel(
    core_ref, own_ref, other_ref, window_ref, table_ref, list_ref, ua_ref, va_ref, out_ref, u_ref, v_ref, rows_ref
):
    second = core_ref[0] == 1

    def extended_of(i, lanes):
        own = own_ref[i, :, lanes].astype(jnp.float32)
        other = other_ref[i, :, lanes].astype(jnp.float32)
        return jnp.concatenate(
            [
                jnp.where(second, other[8:], own[:8]),
                jnp.where(second, own[:8], own[8:]),
                jnp.where(second, own[8:], other[:8]),
            ],
            axis=0,
        )

    u_ref[:128, :] = ua_ref[...]
    v_ref[:128, :] = va_ref[...]
    u_ref[192:, :] = jnp.zeros((64, HALF), jnp.bfloat16)
    v_ref[192:, :] = jnp.zeros((64, HALF), jnp.bfloat16)
    fold_into(u_ref, v_ref, 128, range(INS), 2, 512, extended_of, window_ref)

    low = lax.broadcasted_iota(jnp.int32, (1, 128), 1) < 64
    for q in range(N_FREQ):
        halves = []
        for parity, folded in enumerate((u_ref, v_ref)):
            y = nt_dot(table_ref[q, parity], folded[...])
            re, im = y[:128, :128], y[128:, :128]
            rest = y[:128, 128:] + pltpu.roll(y[128:, 128:], 64, 1)
            first = jnp.where(low, re, pltpu.roll(im, 64, 1))
            last = jnp.where(low, pltpu.roll(re, 64, 1), im)
            halves.append(jnp.concatenate([first, rest, last], axis=1))
        spectra = jnp.concatenate(halves, axis=0).astype(jnp.bfloat16)
        channels = list_ref[q]
        place = (channels & 1) * 128 + ((channels & 255) >> 1)
        place = jnp.concatenate([place[:1], place[1:]], axis=1)
        picks = (lax.broadcasted_iota(jnp.int32, (QUARTER, QUARTER), 0) == place).astype(jnp.float32)
        picked = jnp.dot(picks.T.astype(jnp.bfloat16), spectra, preferred_element_type=jnp.float32)
        for tile in range(3):
            for slot in range(2):
                rows_ref[pl.ds(q * 6 + tile * 2 + slot, N_BLK, stride=N_FREQ * 6), :] = picked[
                    slot * N_BLK : (slot + 1) * N_BLK, tile * 128 : (tile + 1) * 128
                ]
    out_ref[...] = rows_ref[...].astype(jnp.bfloat16)


def own_part(core, own, window, table):
    hbm = pl.BlockSpec(memory_space=pltpu.HBM)
    vmem = pl.BlockSpec(memory_space=pltpu.VMEM)
    pinned = [pltpu.with_memory_space_constraint(x, pltpu.HBM) for x in (own, window, table)]
    half = pltpu.VMEM((128, HALF), jnp.bfloat16)
    return pl.pallas_call(
        own_kernel,
        in_specs=[pl.BlockSpec(memory_space=pltpu.SMEM), hbm, hbm, hbm],
        out_specs=[vmem] * 5,
        out_shape=[half, half, *(pltpu.VMEM(x.shape, x.dtype) for x in (own, window, table))],
        scratch_shapes=[pltpu.SemaphoreType.DMA((6,))],
        compiler_params=pltpu.CompilerParams(vmem_limit_bytes=24 << 20),
        cost_estimate=pl.CostEstimate(flops=10_000_000, bytes_accessed=2_000_000, transcendentals=0),
        name="own",
    )(core, *pinned)


def channel_messages(core, own, other, lists):
    window = jnp.asarray(window_taps())
    table = jnp.asarray(fourier_halves())
    ua, va, own, window, table = own_part(core, own, window, table)
    vmem = pl.BlockSpec(memory_space=pltpu.VMEM)
    return pl.pallas_call(
        channel_kernel,
        in_specs=[pl.BlockSpec(memory_space=pltpu.SMEM)] + [vmem] * 7,
        out_specs=vmem,
        out_shape=jax.ShapeDtypeStruct((N_FREQ * N_BLK * 6, 128), jnp.bfloat16),
        scratch_shapes=[
            pltpu.VMEM((256, HALF), jnp.bfloat16),
            pltpu.VMEM((256, HALF), jnp.bfloat16),
            pltpu.VMEM((N_FREQ * N_BLK * 6, 128), jnp.float32),
        ],
        compiler_params=pltpu.CompilerParams(vmem_limit_bytes=32 << 20),
        name="channels",
    )(core, own, other, window, table, lists, ua, va)


def correlate_kernel(count_ref, got_ref, merge_ref, out_ref, rows_ref, right_all, even_all, odd_all, left_ref, right_ref):
    slot = pl.program_id(0)

    @pl.when(slot == 0)
    def _():
        sign = jnp.where(lax.broadcasted_iota(jnp.int32, (1, 128), 1) < 64, 1.0, -1.0)
        rows_ref[...] = got_ref[...].astype(jnp.float32)
        sources = {}
        for f in range(N_FREQ):
            for tile in range(3):
                start = f * 6 + tile * 2
                sources[f, tile] = jnp.concatenate(
                    [rows_ref[pl.ds(start + j, N_BLK, stride=N_FREQ * 6), :] for j in range(2)], axis=0
                ).astype(jnp.bfloat16)
        base = 0
        for pair, tiles in enumerate(GROUPS):
            depth = N_FREQ * len(tiles) * 128
            parts = [sources[f, tile] for f in range(N_FREQ) for tile in tiles]
            both = jnp.dot(
                jnp.concatenate(parts, axis=1),
                merge_ref[base : base + depth, :],
                preferred_element_type=jnp.float32,
            )
            base += depth
            for h in range(2):
                plain = both[:, h * 128 : (h + 1) * 128]
                turned = pltpu.roll(plain, 64, 1) * sign
                right_all[pl.ds(2 * pair + h, 256, stride=8), :] = plain
                left_all = (even_all, odd_all)[h]
                left_all[pl.ds(2 * pair, 256, stride=8), :] = plain
                left_all[pl.ds(2 * pair + 1, 256, stride=8), :] = turned

    live = slot < count_ref[0, 0]

    @pl.when(live)
    def _():
        def tile_of(ref, tile):
            return ref[pl.ds(pl.multiple_of(slot * 1024 + tile * 64, 64), 64), :].astype(jnp.bfloat16)

        for tile in range(TILES):
            rows = slice(tile * 64, tile * 64 + 64)
            left_ref[rows, :128] = tile_of(even_all, tile)
            left_ref[rows, 128:] = tile_of(odd_all, tile)
            right_ref[rows, :] = tile_of(right_all, tile)
        zero = jnp.zeros((64, 128), jnp.bfloat16)
        for m in range(TILES // 2):
            rhs = []
            for q in (2 * m, 2 * m + 1):
                column = right_ref[q * 64 : (q + 1) * 64, :]
                rhs.append(jnp.concatenate([column, zero], axis=1))
                rhs.append(jnp.concatenate([zero, column], axis=1))
            products = nt_dot(left_ref[: (2 * m + 2) * 64, :], jnp.concatenate(rhs, axis=0))
            for h in range(2):
                q = 2 * m + h
                for p in range(q + 1):
                    t = TILES * p - p * (p - 1) // 2 + q - p
                    piece = products[p * 64 : (p + 1) * 64, h * 128 : (h + 1) * 128]
                    out_ref[0, t] = (piece * (1.0 / 64.0)).astype(jnp.bfloat16)

    @pl.when(jnp.logical_not(live))
    def _():
        out_ref[...] = jnp.zeros(out_ref.shape, out_ref.dtype)


def visibility_tiles(counts, got):
    merge = jnp.asarray(merge_matrices())
    return pl.pallas_call(
        correlate_kernel,
        grid=(2,),
        in_specs=[
            pl.BlockSpec(memory_space=pltpu.SMEM),
            pl.BlockSpec((N_FREQ * N_BLK * 6, 128), lambda j: (0, 0)),
            pl.BlockSpec(merge.shape, lambda j: (0, 0)),
        ],
        out_specs=pl.BlockSpec((1, PAIRS, 64, 128), lambda j: (j, 0, 0, 0)),
        out_shape=jax.ShapeDtypeStruct((2, PAIRS, 64, 128), jnp.bfloat16),
        scratch_shapes=[
            pltpu.VMEM((N_FREQ * N_BLK * 6, 128), jnp.float32),
            pltpu.VMEM((2048, 128), jnp.float32),
            pltpu.VMEM((2048, 128), jnp.float32),
            pltpu.VMEM((2048, 128), jnp.float32),
            pltpu.VMEM((1024, 256), jnp.bfloat16),
            pltpu.VMEM((1024, 128), jnp.bfloat16),
        ],
        compiler_params=pltpu.CompilerParams(vmem_limit_bytes=40 << 20),
        name="correlate",
    )(counts, got, merge)


def shards(samples, channel_lists, channel_counts):
    core = lax.axis_index("core").astype(jnp.int32).reshape(1)
    other = lax.ppermute(samples, "core", [(0, 1), (1, 0)])
    lists = channel_lists.transpose(0, 2, 1)
    messages = channel_messages(core, samples, other, lists)
    got = lax.all_to_all(
        messages.reshape(N_FREQ * N_BLK, 3, 2, 128), ("z_lo", "y", "x", "z_hi", "core"), 0, 0, tiled=True
    ).reshape(N_FREQ * N_BLK * 6, 128)
    tiles = visibility_tiles(channel_counts, got)
    tiles = tiles.reshape(2, PAIRS, 32, 2, 128).transpose(0, 1, 3, 2, 4)
    return tiles.reshape(1, 1, 2, PAIRS, 2, 4096)


def solution(mesh):
    fine = Mesh(mesh.devices.reshape(8, 4, 4, 2, 2), ("z_lo", "y", "x", "z_hi", "core"))
    blk, freq = ("z_lo", "y", "x"), ("z_hi", "core")
    in_specs = (P(blk, freq, None), P(), P(freq, blk))
    out_specs = P(freq, blk, None, None, None, None)
    return jax.shard_map(shards, mesh=fine, in_specs=in_specs, out_specs=out_specs, check_vma=False)
```

```python
import math

import jax
import jax.numpy as jnp
import ml_dtypes
import numpy as np
from jax import lax
from jax.experimental import pallas as pl
from jax.experimental.pallas import tpu as pltpu
from jax.sharding import Mesh, PartitionSpec as P

FRAME = 2048
HALF = 1024
TAPS = 16
INS = 8
OUT_T = 24
QUARTER = 256
N_BLK = 128
N_FREQ = 4
TILES = 16
PAIRS = 136
GROUPS = ((0, 1, 2),) * 4


def window_taps():
    total_len = FRAME * TAPS
    m = np.arange(total_len, dtype=np.float64)
    shaped = np.sinc((m - total_len / 2 + 0.5) / FRAME)
    shaped = shaped * (0.5 - 0.5 * np.cos(2.0 * np.pi * (m + 0.5) / total_len))
    shaped = shaped / np.sqrt(np.sum(shaped * shaped) / FRAME)
    return shaped.reshape(TAPS, FRAME).astype(np.float32)


def fourier_halves():
    channels = np.arange(1024).reshape(4, 128, 2).transpose(0, 2, 1)
    phase = channels[..., None] * np.arange(HALF) % FRAME
    angle = phase * (2.0 * np.pi / FRAME)
    scale = 1.0 / math.sqrt(FRAME)
    both = np.concatenate([np.cos(angle) * scale, -np.sin(angle) * scale], axis=2)
    return both.astype(np.float32).astype(ml_dtypes.bfloat16)


def message_lane(core, i, t, r):
    own = t - 8 * core
    if 0 <= own < 16:
        return own // 8 * 256 + 64 * r + own % 8 * 8 + i
    return 128 + 64 * r + t % 8 * 8 + i


def merge_matrices():
    blocks = []
    for pair, tiles in enumerate(GROUPS):
        block = np.zeros((N_FREQ, len(tiles), 128, 2, 128), np.float32)
        for f in range(N_FREQ):
            for h in range(2):
                for t in range(OUT_T):
                    local = OUT_T * (f % 2) + t
                    if local > 46:
                        continue
                    spectrum = (32 * (f // 2) + local) % 64
                    for r in range(2):
                        lane = message_lane(f % 2, 2 * pair + h, t, r)
                        block[f, tiles.index(lane // 128), lane % 128, h, r * 64 + spectrum] = 1.0
        blocks.append(block.reshape(-1, 256))
    return np.concatenate(blocks).astype(ml_dtypes.bfloat16)


def nt_dot(a, b):
    return lax.dot_general(a, b, (((1,), (1,)), ((), ())), preferred_element_type=jnp.float32)


def spread(block_ref, first, frames, into_ref):
    for i in range(INS):
        for tile in range(FRAME // 128):
            values = block_ref[i, :, tile * 128 : (tile + 1) * 128].astype(jnp.float32)
            into_ref[pl.ds(tile * frames * 8 + i, frames, stride=8), :] = values[first : first + frames]


def fold_into(u_ref, v_ref, row, outputs, terms_of, frame_of, window_ref):
    def one(tile, carry):
        parts = []
        for half in (tile, tile + HALF // 128):
            lanes = pl.ds(pl.multiple_of(half * 128, 128), 128)
            taps = [jnp.broadcast_to(window_ref[k : k + 1, lanes], (8, 128)) for k in range(TAPS)]
            frames = {}
            totals = []
            for t in range(outputs):
                total = jnp.zeros((8, 128), jnp.float32)
                for k, m in terms_of(t):
                    if m not in frames:
                        frames[m] = frame_of(m, half)
                    total = total + taps[k] * frames[m]
                totals.append(total)
            parts.append(totals)
        lanes = pl.ds(pl.multiple_of(tile * 128, 128), 128)
        for t in range(0, outputs, 2):
            low = jnp.concatenate(parts[0][t : t + 2], axis=0)
            high = jnp.concatenate(parts[1][t : t + 2], axis=0)
            u_ref[row + t * 8 : row + t * 8 + 16, lanes] = (low + high).astype(jnp.bfloat16)
            v_ref[row + t * 8 : row + t * 8 + 16, lanes] = (low - high).astype(jnp.bfloat16)
        return carry

    lax.fori_loop(0, HALF // 128, one, 0)


def own_kernel(core_ref, own_hbm, window_hbm, table_hbm, u_ref, v_ref, frames_ref, window_ref, table_ref, own_ref, sems):
    copies = [
        pltpu.make_async_copy(own_hbm, own_ref, sems.at[0]),
        pltpu.make_async_copy(window_hbm, window_ref, sems.at[1]),
        pltpu.make_async_copy(table_hbm, table_ref, sems.at[2]),
    ]
    for copy in copies:
        copy.start()
    copies[0].wait()
    spread(own_ref, 0, 16, frames_ref)
    copies[1].wait()

    def frame_of(m, tile):
        return frames_ref[pl.ds(pl.multiple_of(tile * 128 + m * 8, 8), 8), :]

    second = core_ref[0] == 1

    @pl.when(jnp.logical_not(second))
    def _():
        fold_into(u_ref, v_ref, 0, 16, lambda t: [(15 - t + m, m) for m in range(t + 1)], frame_of, window_ref)

    @pl.when(second)
    def _():
        fold_into(u_ref, v_ref, 0, 16, lambda t: [(m - t - 1, m) for m in range(t + 1, 16)], frame_of, window_ref)

    copies[2].wait()


def channel_kernel(
    core_ref, frames_ref, other_ref, window_ref, table_ref, list_ref, ua_ref, va_ref, out_ref, u_ref, v_ref, rows_ref, more_ref
):
    second = core_ref[0] == 1

    def own_frame(m, tile):
        return frames_ref[pl.ds(pl.multiple_of(tile * 128 + m * 8, 8), 8), :]

    def more_frame(m, tile):
        return more_ref[pl.ds(pl.multiple_of(tile * 64 + m * 8, 8), 8), :]

    def terms_of(t):
        return [(k, t + 1 + k) for k in range(TAPS)]

    @pl.when(jnp.logical_not(second))
    def _():
        spread(other_ref, 0, 8, more_ref)

        def frame_of(m, tile):
            return own_frame(m, tile) if m < 16 else more_frame(m - 16, tile)

        fold_into(u_ref, v_ref, 128, 8, terms_of, frame_of, window_ref)

    @pl.when(second)
    def _():
        spread(other_ref, 8, 8, more_ref)

        def frame_of(m, tile):
            return more_frame(m, tile) if m < 8 else own_frame(m - 8, tile)

        fold_into(u_ref, v_ref, 128, 8, terms_of, frame_of, window_ref)

    u_ref[:128, :] = ua_ref[...]
    v_ref[:128, :] = va_ref[...]
    u_ref[192:, :] = jnp.zeros((64, HALF), jnp.bfloat16)
    v_ref[192:, :] = jnp.zeros((64, HALF), jnp.bfloat16)

    low = lax.broadcasted_iota(jnp.int32, (1, 128), 1) < 64
    whole = [
        nt_dot(table_ref[:, parity].reshape(4 * 256, HALF), folded[...])
        for parity, folded in enumerate((u_ref, v_ref))
    ]
    for q in range(N_FREQ):
        halves = []
        for parity in range(2):
            y = whole[parity][q * 256 : (q + 1) * 256]
            re, im = y[:128, :128], y[128:, :128]
            rest = y[:128, 128:] + pltpu.roll(y[128:, 128:], 64, 1)
            first = jnp.where(low, re, pltpu.roll(im, 64, 1))
            last = jnp.where(low, pltpu.roll(re, 64, 1), im)
            halves.append(jnp.concatenate([first, rest, last], axis=1))
        spectra = jnp.concatenate(halves, axis=0).astype(jnp.bfloat16)
        channels = list_ref[q]
        place = (channels & 1) * 128 + ((channels & 255) >> 1)
        place = jnp.concatenate([place[:1], place[1:]], axis=1)
        picks = (lax.broadcasted_iota(jnp.int32, (QUARTER, QUARTER), 0) == place).astype(jnp.float32)
        picked = jnp.dot(picks.T.astype(jnp.bfloat16), spectra, preferred_element_type=jnp.float32)
        for tile in range(3):
            for slot in range(2):
                rows_ref[pl.ds(q * 6 + tile * 2 + slot, N_BLK, stride=N_FREQ * 6), :] = picked[
                    slot * N_BLK : (slot + 1) * N_BLK, tile * 128 : (tile + 1) * 128
                ]
    out_ref[...] = rows_ref[...].astype(jnp.bfloat16)


def own_part(core, own, window, table):
    hbm = pl.BlockSpec(memory_space=pltpu.HBM)
    vmem = pl.BlockSpec(memory_space=pltpu.VMEM)
    pinned = [pltpu.with_memory_space_constraint(x, pltpu.HBM) for x in (own, window, table)]
    half = pltpu.VMEM((128, HALF), jnp.bfloat16)
    return pl.pallas_call(
        own_kernel,
        in_specs=[pl.BlockSpec(memory_space=pltpu.SMEM), hbm, hbm, hbm],
        out_specs=[vmem] * 5,
        out_shape=[
            half,
            half,
            pltpu.VMEM((FRAME, 128), jnp.float32),
            pltpu.VMEM(window.shape, jnp.float32),
            pltpu.VMEM(table.shape, jnp.bfloat16),
        ],
        scratch_shapes=[pltpu.VMEM(own.shape, jnp.bfloat16), pltpu.SemaphoreType.DMA((3,))],
        compiler_params=pltpu.CompilerParams(vmem_limit_bytes=24 << 20),
        cost_estimate=pl.CostEstimate(flops=10_000_000, bytes_accessed=2_000_000, transcendentals=0),
        name="own",
    )(core, *pinned)


def channel_messages(core, own, other, lists):
    window = jnp.asarray(window_taps())
    table = jnp.asarray(fourier_halves())
    ua, va, frames, window, table = own_part(core, own, window, table)
    vmem = pl.BlockSpec(memory_space=pltpu.VMEM)
    return pl.pallas_call(
        channel_kernel,
        in_specs=[pl.BlockSpec(memory_space=pltpu.SMEM)] + [vmem] * 7,
        out_specs=vmem,
        out_shape=jax.ShapeDtypeStruct((N_FREQ * N_BLK * 6, 128), jnp.bfloat16),
        scratch_shapes=[
            pltpu.VMEM((256, HALF), jnp.bfloat16),
            pltpu.VMEM((256, HALF), jnp.bfloat16),
            pltpu.VMEM((N_FREQ * N_BLK * 6, 128), jnp.float32),
            pltpu.VMEM((FRAME // 2, 128), jnp.float32),
        ],
        compiler_params=pltpu.CompilerParams(vmem_limit_bytes=32 << 20),
        name="channels",
    )(core, frames, other, window, table, lists, ua, va)


def correlate_kernel(count_ref, got_ref, merge_ref, out_ref, rows_ref, right_all, even_all, odd_all, left_ref, right_ref):
    slot = pl.program_id(0)

    @pl.when(slot == 0)
    def _():
        sign = jnp.where(lax.broadcasted_iota(jnp.int32, (1, 128), 1) < 64, 1.0, -1.0)
        rows_ref[...] = got_ref[...].astype(jnp.float32)
        sources = {}
        for f in range(N_FREQ):
            for tile in range(3):
                start = f * 6 + tile * 2
                sources[f, tile] = jnp.concatenate(
                    [rows_ref[pl.ds(start + j, N_BLK, stride=N_FREQ * 6), :] for j in range(2)], axis=0
                ).astype(jnp.bfloat16)
        base = 0
        for pair, tiles in enumerate(GROUPS):
            depth = N_FREQ * len(tiles) * 128
            parts = [sources[f, tile] for f in range(N_FREQ) for tile in tiles]
            both = jnp.dot(
                jnp.concatenate(parts, axis=1),
                merge_ref[base : base + depth, :],
                preferred_element_type=jnp.float32,
            )
            base += depth
            for h in range(2):
                plain = both[:, h * 128 : (h + 1) * 128]
                turned = pltpu.roll(plain, 64, 1) * sign
                right_all[pl.ds(2 * pair + h, 256, stride=8), :] = plain
                left_all = (even_all, odd_all)[h]
                left_all[pl.ds(2 * pair, 256, stride=8), :] = plain
                left_all[pl.ds(2 * pair + 1, 256, stride=8), :] = turned

    live = slot < count_ref[0, 0]

    @pl.when(live)
    def _():
        def tile_of(ref, tile):
            return ref[pl.ds(pl.multiple_of(slot * 1024 + tile * 64, 64), 64), :].astype(jnp.bfloat16)

        for tile in range(TILES):
            rows = slice(tile * 64, tile * 64 + 64)
            left_ref[rows, :128] = tile_of(even_all, tile)
            left_ref[rows, 128:] = tile_of(odd_all, tile)
            right_ref[rows, :] = tile_of(right_all, tile)
        zero = jnp.zeros((64, 128), jnp.bfloat16)
        for m in range(TILES // 2):
            rhs = []
            for q in (2 * m, 2 * m + 1):
                column = right_ref[q * 64 : (q + 1) * 64, :]
                rhs.append(jnp.concatenate([column, zero], axis=1))
                rhs.append(jnp.concatenate([zero, column], axis=1))
            products = nt_dot(left_ref[: (2 * m + 2) * 64, :], jnp.concatenate(rhs, axis=0))
            for h in range(2):
                q = 2 * m + h
                for p in range(q + 1):
                    t = TILES * p - p * (p - 1) // 2 + q - p
                    piece = products[p * 64 : (p + 1) * 64, h * 128 : (h + 1) * 128]
                    out_ref[0, t] = (piece * (1.0 / 64.0)).astype(jnp.bfloat16)

    @pl.when(jnp.logical_not(live))
    def _():
        out_ref[...] = jnp.zeros(out_ref.shape, out_ref.dtype)


def visibility_tiles(counts, got):
    merge = jnp.asarray(merge_matrices())
    return pl.pallas_call(
        correlate_kernel,
        grid=(2,),
        in_specs=[
            pl.BlockSpec(memory_space=pltpu.SMEM),
            pl.BlockSpec((N_FREQ * N_BLK * 6, 128), lambda j: (0, 0)),
            pl.BlockSpec(merge.shape, lambda j: (0, 0)),
        ],
        out_specs=pl.BlockSpec((1, PAIRS, 64, 128), lambda j: (j, 0, 0, 0)),
        out_shape=jax.ShapeDtypeStruct((2, PAIRS, 64, 128), jnp.bfloat16),
        scratch_shapes=[
            pltpu.VMEM((N_FREQ * N_BLK * 6, 128), jnp.float32),
            pltpu.VMEM((2048, 128), jnp.float32),
            pltpu.VMEM((2048, 128), jnp.float32),
            pltpu.VMEM((2048, 128), jnp.float32),
            pltpu.VMEM((1024, 256), jnp.bfloat16),
            pltpu.VMEM((1024, 128), jnp.bfloat16),
        ],
        compiler_params=pltpu.CompilerParams(vmem_limit_bytes=40 << 20),
        name="correlate",
    )(counts, got, merge)


def shards(samples, channel_lists, channel_counts):
    core = lax.axis_index("core").astype(jnp.int32).reshape(1)
    other = lax.ppermute(samples, "core", [(0, 1), (1, 0)])
    lists = channel_lists.transpose(0, 2, 1)
    messages = channel_messages(core, samples, other, lists)
    got = lax.all_to_all(
        messages.reshape(N_FREQ * N_BLK, 3, 2, 128), ("z_lo", "y", "x", "z_hi", "core"), 0, 0, tiled=True
    ).reshape(N_FREQ * N_BLK * 6, 128)
    tiles = visibility_tiles(channel_counts, got)
    tiles = tiles.reshape(2, PAIRS, 32, 2, 128).transpose(0, 1, 3, 2, 4)
    return tiles.reshape(1, 1, 2, PAIRS, 2, 4096)


def solution(mesh):
    fine = Mesh(mesh.devices.reshape(8, 4, 4, 2, 2), ("z_lo", "y", "x", "z_hi", "core"))
    blk, freq = ("z_lo", "y", "x"), ("z_hi", "core")
    in_specs = (P(blk, freq, None), P(), P(freq, blk))
    out_specs = P(freq, blk, None, None, None, None)
    return jax.shard_map(shards, mesh=fine, in_specs=in_specs, out_specs=out_specs, check_vma=False)
```

```python
import math

import jax
import jax.numpy as jnp
import ml_dtypes
import numpy as np
from jax import lax
from jax.experimental import pallas as pl
from jax.experimental.pallas import tpu as pltpu
from jax.sharding import Mesh, PartitionSpec as P

FRAME = 2048
HALF = 1024
TAPS = 16
INS = 8
OUT_T = 24
QUARTER = 256
N_BLK = 128
N_FREQ = 4
TILES = 16
PAIRS = 136
GROUPS = ((0, 1), (0, 1), (1, 2), (1, 2))


def window_taps():
    total_len = FRAME * TAPS
    m = np.arange(total_len, dtype=np.float64)
    shaped = np.sinc((m - total_len / 2 + 0.5) / FRAME)
    shaped = shaped * (0.5 - 0.5 * np.cos(2.0 * np.pi * (m + 0.5) / total_len))
    shaped = shaped / np.sqrt(np.sum(shaped * shaped) / FRAME)
    return shaped.reshape(TAPS, FRAME).astype(np.float32)


def fourier_halves():
    channels = np.arange(1024).reshape(4, 128, 2).transpose(0, 2, 1)
    phase = channels[..., None] * np.arange(HALF) % FRAME
    angle = phase * (2.0 * np.pi / FRAME)
    scale = 1.0 / math.sqrt(FRAME)
    both = np.concatenate([np.cos(angle) * scale, -np.sin(angle) * scale], axis=2)
    return both.astype(np.float32).astype(ml_dtypes.bfloat16)


def message_lane(core, i, t, r):
    own = t - 8 * core
    if 0 <= own < 16:
        return i // 4 * 256 + 64 * r + own * 4 + i % 4
    return 128 + 64 * r + t % 8 * 8 + i


def merge_matrices():
    blocks = []
    for pair, tiles in enumerate(GROUPS):
        block = np.zeros((N_FREQ, len(tiles), 128, 2, 128), np.float32)
        for f in range(N_FREQ):
            for h in range(2):
                for t in range(OUT_T):
                    local = OUT_T * (f % 2) + t
                    if local > 46:
                        continue
                    spectrum = (32 * (f // 2) + local) % 64
                    for r in range(2):
                        lane = message_lane(f % 2, 2 * pair + h, t, r)
                        block[f, tiles.index(lane // 128), lane % 128, h, r * 64 + spectrum] = 1.0
        blocks.append(block.reshape(-1, 256))
    return np.concatenate(blocks).astype(ml_dtypes.bfloat16)


def nt_dot(a, b):
    return lax.dot_general(a, b, (((1,), (1,)), ((), ())), preferred_element_type=jnp.float32)


def spread(block_ref, first, frames, into_ref):
    for i in range(INS):
        for tile in range(FRAME // 128):
            values = block_ref[i, :, tile * 128 : (tile + 1) * 128].astype(jnp.float32)
            into_ref[pl.ds(tile * frames * 8 + i, frames, stride=8), :] = values[first : first + frames]


def by_fours(rows):
    first = lax.broadcasted_iota(jnp.int32, (8, 1), 0) < 4
    low = [jnp.where(first, a, pltpu.roll(b, 4, 0)) for a, b in zip(rows[::2], rows[1::2])]
    high = [jnp.where(first, pltpu.roll(a, 4, 0), b) for a, b in zip(rows[::2], rows[1::2])]
    return low + high


def fold_into(u_ref, v_ref, row, outputs, terms_of, frame_of, window_ref, order=list):
    def one(tile, carry):
        parts = []
        for half in (tile, tile + HALF // 128):
            lanes = pl.ds(pl.multiple_of(half * 128, 128), 128)
            taps = [jnp.broadcast_to(window_ref[k : k + 1, lanes], (8, 128)) for k in range(TAPS)]
            frames = {}
            totals = []
            for t in range(outputs):
                total = jnp.zeros((8, 128), jnp.float32)
                for k, m in terms_of(t):
                    if m not in frames:
                        frames[m] = frame_of(m, half)
                    total = total + taps[k] * frames[m]
                totals.append(total)
            parts.append(totals)
        lanes = pl.ds(pl.multiple_of(tile * 128, 128), 128)
        sums = order([low + high for low, high in zip(*parts)])
        differences = order([low - high for low, high in zip(*parts)])
        for t in range(0, outputs, 2):
            rows = slice(row + t * 8, row + t * 8 + 16)
            u_ref[rows, lanes] = jnp.concatenate(sums[t : t + 2], axis=0).astype(jnp.bfloat16)
            v_ref[rows, lanes] = jnp.concatenate(differences[t : t + 2], axis=0).astype(jnp.bfloat16)
        return carry

    lax.fori_loop(0, HALF // 128, one, 0)


def own_kernel(core_ref, own_hbm, window_hbm, table_hbm, u_ref, v_ref, frames_ref, window_ref, table_ref, own_ref, sems):
    copies = [
        pltpu.make_async_copy(own_hbm, own_ref, sems.at[0]),
        pltpu.make_async_copy(window_hbm, window_ref, sems.at[1]),
        pltpu.make_async_copy(table_hbm, table_ref, sems.at[2]),
    ]
    for copy in copies:
        copy.start()
    copies[0].wait()
    spread(own_ref, 0, 16, frames_ref)
    copies[1].wait()

    def frame_of(m, tile):
        return frames_ref[pl.ds(pl.multiple_of(tile * 128 + m * 8, 8), 8), :]

    second = core_ref[0] == 1

    @pl.when(jnp.logical_not(second))
    def _():
        fold_into(u_ref, v_ref, 0, 16, lambda t: [(15 - t + m, m) for m in range(t + 1)], frame_of, window_ref, by_fours)

    @pl.when(second)
    def _():
        fold_into(u_ref, v_ref, 0, 16, lambda t: [(m - t - 1, m) for m in range(t + 1, 16)], frame_of, window_ref, by_fours)

    copies[2].wait()


def channel_kernel(
    core_ref, frames_ref, other_ref, window_ref, table_ref, list_ref, ua_ref, va_ref, out_ref, u_ref, v_ref, rows_ref, more_ref
):
    second = core_ref[0] == 1

    def own_frame(m, tile):
        return frames_ref[pl.ds(pl.multiple_of(tile * 128 + m * 8, 8), 8), :]

    def more_frame(m, tile):
        return more_ref[pl.ds(pl.multiple_of(tile * 64 + m * 8, 8), 8), :]

    def terms_of(t):
        return [(k, t + 1 + k) for k in range(TAPS)]

    @pl.when(jnp.logical_not(second))
    def _():
        spread(other_ref, 0, 8, more_ref)

        def frame_of(m, tile):
            return own_frame(m, tile) if m < 16 else more_frame(m - 16, tile)

        fold_into(u_ref, v_ref, 128, 8, terms_of, frame_of, window_ref)

    @pl.when(second)
    def _():
        spread(other_ref, 8, 8, more_ref)

        def frame_of(m, tile):
            return more_frame(m, tile) if m < 8 else own_frame(m - 8, tile)

        fold_into(u_ref, v_ref, 128, 8, terms_of, frame_of, window_ref)

    u_ref[:128, :] = ua_ref[...]
    v_ref[:128, :] = va_ref[...]
    u_ref[192:, :] = jnp.zeros((64, HALF), jnp.bfloat16)
    v_ref[192:, :] = jnp.zeros((64, HALF), jnp.bfloat16)

    low = lax.broadcasted_iota(jnp.int32, (1, 128), 1) < 64
    whole = [
        nt_dot(table_ref[:, parity].reshape(4 * 256, HALF), folded[...])
        for parity, folded in enumerate((u_ref, v_ref))
    ]
    for q in range(N_FREQ):
        halves = []
        for parity in range(2):
            y = whole[parity][q * 256 : (q + 1) * 256]
            re, im = y[:128, :128], y[128:, :128]
            rest = y[:128, 128:] + pltpu.roll(y[128:, 128:], 64, 1)
            first = jnp.where(low, re, pltpu.roll(im, 64, 1))
            last = jnp.where(low, pltpu.roll(re, 64, 1), im)
            halves.append(jnp.concatenate([first, rest, last], axis=1))
        spectra = jnp.concatenate(halves, axis=0).astype(jnp.bfloat16)
        channels = list_ref[q]
        place = (channels & 1) * 128 + ((channels & 255) >> 1)
        place = jnp.concatenate([place[:1], place[1:]], axis=1)
        picks = (lax.broadcasted_iota(jnp.int32, (QUARTER, QUARTER), 0) == place).astype(jnp.float32)
        picked = jnp.dot(picks.T.astype(jnp.bfloat16), spectra, preferred_element_type=jnp.float32)
        for tile in range(3):
            for slot in range(2):
                rows_ref[pl.ds(q * 6 + tile * 2 + slot, N_BLK, stride=N_FREQ * 6), :] = picked[
                    slot * N_BLK : (slot + 1) * N_BLK, tile * 128 : (tile + 1) * 128
                ]
    out_ref[...] = rows_ref[...].astype(jnp.bfloat16)


def own_part(core, own, window, table):
    hbm = pl.BlockSpec(memory_space=pltpu.HBM)
    vmem = pl.BlockSpec(memory_space=pltpu.VMEM)
    pinned = [pltpu.with_memory_space_constraint(x, pltpu.HBM) for x in (own, window, table)]
    half = pltpu.VMEM((128, HALF), jnp.bfloat16)
    return pl.pallas_call(
        own_kernel,
        in_specs=[pl.BlockSpec(memory_space=pltpu.SMEM), hbm, hbm, hbm],
        out_specs=[vmem] * 5,
        out_shape=[
            half,
            half,
            pltpu.VMEM((FRAME, 128), jnp.float32),
            pltpu.VMEM(window.shape, jnp.float32),
            pltpu.VMEM(table.shape, jnp.bfloat16),
        ],
        scratch_shapes=[pltpu.VMEM(own.shape, jnp.bfloat16), pltpu.SemaphoreType.DMA((3,))],
        compiler_params=pltpu.CompilerParams(vmem_limit_bytes=24 << 20),
        cost_estimate=pl.CostEstimate(flops=10_000_000, bytes_accessed=2_000_000, transcendentals=0),
        name="own",
    )(core, *pinned)


def channel_messages(core, own, other, lists):
    window = jnp.asarray(window_taps())
    table = jnp.asarray(fourier_halves())
    ua, va, frames, window, table = own_part(core, own, window, table)
    vmem = pl.BlockSpec(memory_space=pltpu.VMEM)
    return pl.pallas_call(
        channel_kernel,
        in_specs=[pl.BlockSpec(memory_space=pltpu.SMEM)] + [vmem] * 7,
        out_specs=vmem,
        out_shape=jax.ShapeDtypeStruct((N_FREQ * N_BLK * 6, 128), jnp.bfloat16),
        scratch_shapes=[
            pltpu.VMEM((256, HALF), jnp.bfloat16),
            pltpu.VMEM((256, HALF), jnp.bfloat16),
            pltpu.VMEM((N_FREQ * N_BLK * 6, 128), jnp.float32),
            pltpu.VMEM((FRAME // 2, 128), jnp.float32),
        ],
        compiler_params=pltpu.CompilerParams(vmem_limit_bytes=32 << 20),
        name="channels",
    )(core, frames, other, window, table, lists, ua, va)


def correlate_kernel(count_ref, got_ref, merge_ref, out_ref, rows_ref, right_all, even_all, odd_all, left_ref, right_ref):
    slot = pl.program_id(0)

    @pl.when(slot == 0)
    def _():
        sign = jnp.where(lax.broadcasted_iota(jnp.int32, (1, 128), 1) < 64, 1.0, -1.0)
        rows_ref[...] = got_ref[...].astype(jnp.float32)
        sources = {}
        for f in range(N_FREQ):
            for tile in range(3):
                start = f * 6 + tile * 2
                sources[f, tile] = jnp.concatenate(
                    [rows_ref[pl.ds(start + j, N_BLK, stride=N_FREQ * 6), :] for j in range(2)], axis=0
                ).astype(jnp.bfloat16)
        base = 0
        for pair, tiles in enumerate(GROUPS):
            depth = N_FREQ * len(tiles) * 128
            parts = [sources[f, tile] for f in range(N_FREQ) for tile in tiles]
            both = jnp.dot(
                jnp.concatenate(parts, axis=1),
                merge_ref[base : base + depth, :],
                preferred_element_type=jnp.float32,
            )
            base += depth
            for h in range(2):
                plain = both[:, h * 128 : (h + 1) * 128]
                turned = pltpu.roll(plain, 64, 1) * sign
                right_all[pl.ds(2 * pair + h, 256, stride=8), :] = plain
                left_all = (even_all, odd_all)[h]
                left_all[pl.ds(2 * pair, 256, stride=8), :] = plain
                left_all[pl.ds(2 * pair + 1, 256, stride=8), :] = turned

    live = slot < count_ref[0, 0]

    @pl.when(live)
    def _():
        def tile_of(ref, tile):
            return ref[pl.ds(pl.multiple_of(slot * 1024 + tile * 64, 64), 64), :].astype(jnp.bfloat16)

        for tile in range(TILES):
            rows = slice(tile * 64, tile * 64 + 64)
            left_ref[rows, :128] = tile_of(even_all, tile)
            left_ref[rows, 128:] = tile_of(odd_all, tile)
            right_ref[rows, :] = tile_of(right_all, tile)
        zero = jnp.zeros((64, 128), jnp.bfloat16)
        for m in range(TILES // 2):
            rhs = []
            for q in (2 * m, 2 * m + 1):
                column = right_ref[q * 64 : (q + 1) * 64, :]
                rhs.append(jnp.concatenate([column, zero], axis=1))
                rhs.append(jnp.concatenate([zero, column], axis=1))
            products = nt_dot(left_ref[: (2 * m + 2) * 64, :], jnp.concatenate(rhs, axis=0))
            for h in range(2):
                q = 2 * m + h
                for p in range(q + 1):
                    t = TILES * p - p * (p - 1) // 2 + q - p
                    piece = products[p * 64 : (p + 1) * 64, h * 128 : (h + 1) * 128]
                    out_ref[0, t] = (piece * (1.0 / 64.0)).astype(jnp.bfloat16)

    @pl.when(jnp.logical_not(live))
    def _():
        out_ref[...] = jnp.zeros(out_ref.shape, out_ref.dtype)


def visibility_tiles(counts, got):
    merge = jnp.asarray(merge_matrices())
    return pl.pallas_call(
        correlate_kernel,
        grid=(2,),
        in_specs=[
            pl.BlockSpec(memory_space=pltpu.SMEM),
            pl.BlockSpec((N_FREQ * N_BLK * 6, 128), lambda j: (0, 0)),
            pl.BlockSpec(merge.shape, lambda j: (0, 0)),
        ],
        out_specs=pl.BlockSpec((1, PAIRS, 64, 128), lambda j: (j, 0, 0, 0)),
        out_shape=jax.ShapeDtypeStruct((2, PAIRS, 64, 128), jnp.bfloat16),
        scratch_shapes=[
            pltpu.VMEM((N_FREQ * N_BLK * 6, 128), jnp.float32),
            pltpu.VMEM((2048, 128), jnp.float32),
            pltpu.VMEM((2048, 128), jnp.float32),
            pltpu.VMEM((2048, 128), jnp.float32),
            pltpu.VMEM((1024, 256), jnp.bfloat16),
            pltpu.VMEM((1024, 128), jnp.bfloat16),
        ],
        compiler_params=pltpu.CompilerParams(vmem_limit_bytes=40 << 20),
        name="correlate",
    )(counts, got, merge)


def shards(samples, channel_lists, channel_counts):
    core = lax.axis_index("core").astype(jnp.int32).reshape(1)
    other = lax.ppermute(samples, "core", [(0, 1), (1, 0)])
    lists = channel_lists.transpose(0, 2, 1)
    messages = channel_messages(core, samples, other, lists)
    got = lax.all_to_all(
        messages.reshape(N_FREQ * N_BLK, 3, 2, 128), ("z_lo", "y", "x", "z_hi", "core"), 0, 0, tiled=True
    ).reshape(N_FREQ * N_BLK * 6, 128)
    tiles = visibility_tiles(channel_counts, got)
    tiles = tiles.reshape(2, PAIRS, 32, 2, 128).transpose(0, 1, 3, 2, 4)
    return tiles.reshape(1, 1, 2, PAIRS, 2, 4096)


def solution(mesh):
    fine = Mesh(mesh.devices.reshape(8, 4, 4, 2, 2), ("z_lo", "y", "x", "z_hi", "core"))
    blk, freq = ("z_lo", "y", "x"), ("z_hi", "core")
    in_specs = (P(blk, freq, None), P(), P(freq, blk))
    out_specs = P(freq, blk, None, None, None, None)
    return jax.shard_map(shards, mesh=fine, in_specs=in_specs, out_specs=out_specs, check_vma=False)
```

```python
import math

import jax
import jax.numpy as jnp
import ml_dtypes
import numpy as np
from jax import lax
from jax.experimental import pallas as pl
from jax.experimental.pallas import tpu as pltpu
from jax.sharding import Mesh, PartitionSpec as P

FRAME = 2048
HALF = 1024
TAPS = 16
INS = 8
OUT_T = 24
QUARTER = 256
N_BLK = 128
N_FREQ = 4
TILES = 16
PAIRS = 136
GROUPS = ((0, 1), (0, 1), (1, 2), (1, 2))


def window_taps():
    total_len = FRAME * TAPS
    m = np.arange(total_len, dtype=np.float64)
    shaped = np.sinc((m - total_len / 2 + 0.5) / FRAME)
    shaped = shaped * (0.5 - 0.5 * np.cos(2.0 * np.pi * (m + 0.5) / total_len))
    shaped = shaped / np.sqrt(np.sum(shaped * shaped) / FRAME)
    return shaped.reshape(TAPS, FRAME).astype(np.float32)


def fourier_halves():
    channels = np.arange(1024).reshape(4, 128, 2).transpose(0, 2, 1)
    phase = channels[..., None] * np.arange(HALF) % FRAME
    angle = phase * (2.0 * np.pi / FRAME)
    scale = 1.0 / math.sqrt(FRAME)
    both = np.concatenate([np.cos(angle) * scale, -np.sin(angle) * scale], axis=2)
    return both.astype(np.float32).astype(ml_dtypes.bfloat16)


def message_lane(core, i, t, r):
    own = t - 8 * core
    if 0 <= own < 16:
        return i // 4 * 256 + 64 * r + own * 4 + i % 4
    return 128 + 64 * r + t % 8 * 8 + i


def merge_matrices():
    blocks = []
    for pair, tiles in enumerate(GROUPS):
        block = np.zeros((N_FREQ, len(tiles), 128, 2, 128), np.float32)
        for f in range(N_FREQ):
            for h in range(2):
                for t in range(OUT_T):
                    local = OUT_T * (f % 2) + t
                    if local > 46:
                        continue
                    spectrum = (32 * (f // 2) + local) % 64
                    for r in range(2):
                        lane = message_lane(f % 2, 2 * pair + h, t, r)
                        block[f, tiles.index(lane // 128), lane % 128, h, r * 64 + spectrum] = 1.0
        blocks.append(block.reshape(-1, 256))
    return np.concatenate(blocks).astype(ml_dtypes.bfloat16)


def nt_dot(a, b):
    return lax.dot_general(a, b, (((1,), (1,)), ((), ())), preferred_element_type=jnp.float32)


def spread(block_ref, first, frames, into_ref):
    for i in range(INS):
        for tile in range(FRAME // 128):
            values = block_ref[i, :, tile * 128 : (tile + 1) * 128].astype(jnp.float32)
            into_ref[pl.ds(tile * frames * 8 + i, frames, stride=8), :] = values[first : first + frames]


def by_fours(rows):
    first = lax.broadcasted_iota(jnp.int32, (8, 1), 0) < 4
    low = [jnp.where(first, a, pltpu.roll(b, 4, 0)) for a, b in zip(rows[::2], rows[1::2])]
    high = [jnp.where(first, pltpu.roll(a, 4, 0), b) for a, b in zip(rows[::2], rows[1::2])]
    return low + high


def fold_into(u_ref, v_ref, row, outputs, terms_of, frame_of, window_ref, order=list):
    def one(tile, carry):
        parts = []
        for half in (tile, tile + HALF // 128):
            lanes = pl.ds(pl.multiple_of(half * 128, 128), 128)
            taps = [jnp.broadcast_to(window_ref[k : k + 1, lanes], (8, 128)) for k in range(TAPS)]
            frames = {}
            totals = []
            for t in range(outputs):
                total = jnp.zeros((8, 128), jnp.float32)
                for k, m in terms_of(t):
                    if m not in frames:
                        frames[m] = frame_of(m, half)
                    total = total + taps[k] * frames[m]
                totals.append(total)
            parts.append(totals)
        lanes = pl.ds(pl.multiple_of(tile * 128, 128), 128)
        sums = order([low + high for low, high in zip(*parts)])
        differences = order([low - high for low, high in zip(*parts)])
        for t in range(0, outputs, 2):
            rows = slice(row + t * 8, row + t * 8 + 16)
            u_ref[rows, lanes] = jnp.concatenate(sums[t : t + 2], axis=0).astype(jnp.bfloat16)
            v_ref[rows, lanes] = jnp.concatenate(differences[t : t + 2], axis=0).astype(jnp.bfloat16)
        return carry

    lax.fori_loop(0, HALF // 128, one, 0)


def own_kernel(core_ref, own_hbm, window_hbm, table_hbm, u_ref, v_ref, frames_ref, window_ref, table_ref, own_ref, sems):
    copies = [
        pltpu.make_async_copy(own_hbm, own_ref, sems.at[0]),
        pltpu.make_async_copy(window_hbm, window_ref, sems.at[1]),
        pltpu.make_async_copy(table_hbm, table_ref, sems.at[2]),
    ]
    for copy in copies:
        copy.start()
    copies[0].wait()
    spread(own_ref, 0, 16, frames_ref)
    copies[1].wait()

    def frame_of(m, tile):
        return frames_ref[pl.ds(pl.multiple_of(tile * 128 + m * 8, 8), 8), :]

    second = core_ref[0] == 1

    @pl.when(jnp.logical_not(second))
    def _():
        fold_into(u_ref, v_ref, 0, 16, lambda t: [(15 - t + m, m) for m in range(t + 1)], frame_of, window_ref, by_fours)

    @pl.when(second)
    def _():
        fold_into(u_ref, v_ref, 0, 16, lambda t: [(m - t - 1, m) for m in range(t + 1, 16)], frame_of, window_ref, by_fours)

    copies[2].wait()


def channel_kernel(
    core_ref, frames_ref, other_ref, window_ref, table_ref, list_ref, ua_ref, va_ref, out_hbm, u_ref, v_ref, rows_ref, more_ref, out_ref, sems
):
    second = core_ref[0] == 1

    def own_frame(m, tile):
        return frames_ref[pl.ds(pl.multiple_of(tile * 128 + m * 8, 8), 8), :]

    def more_frame(m, tile):
        return more_ref[pl.ds(pl.multiple_of(tile * 64 + m * 8, 8), 8), :]

    def terms_of(t):
        return [(k, t + 1 + k) for k in range(TAPS)]

    @pl.when(jnp.logical_not(second))
    def _():
        spread(other_ref, 0, 8, more_ref)

        def frame_of(m, tile):
            return own_frame(m, tile) if m < 16 else more_frame(m - 16, tile)

        fold_into(u_ref, v_ref, 128, 8, terms_of, frame_of, window_ref)

    @pl.when(second)
    def _():
        spread(other_ref, 8, 8, more_ref)

        def frame_of(m, tile):
            return more_frame(m, tile) if m < 8 else own_frame(m - 8, tile)

        fold_into(u_ref, v_ref, 128, 8, terms_of, frame_of, window_ref)

    u_ref[:128, :] = ua_ref[...]
    v_ref[:128, :] = va_ref[...]
    u_ref[192:, :] = jnp.zeros((64, HALF), jnp.bfloat16)
    v_ref[192:, :] = jnp.zeros((64, HALF), jnp.bfloat16)

    low = lax.broadcasted_iota(jnp.int32, (1, 128), 1) < 64
    whole = [
        nt_dot(table_ref[:, parity].reshape(4 * 256, HALF), folded[...])
        for parity, folded in enumerate((u_ref, v_ref))
    ]
    copies = []
    for q in range(N_FREQ):
        halves = []
        for parity in range(2):
            y = whole[parity][q * 256 : (q + 1) * 256]
            re, im = y[:128, :128], y[128:, :128]
            rest = y[:128, 128:] + pltpu.roll(y[128:, 128:], 64, 1)
            first = jnp.where(low, re, pltpu.roll(im, 64, 1))
            last = jnp.where(low, pltpu.roll(re, 64, 1), im)
            halves.append(jnp.concatenate([first, rest, last], axis=1))
        spectra = jnp.concatenate(halves, axis=0).astype(jnp.bfloat16)
        channels = list_ref[q]
        place = (channels & 1) * 128 + ((channels & 255) >> 1)
        place = jnp.concatenate([place[:1], place[1:]], axis=1)
        picks = (lax.broadcasted_iota(jnp.int32, (QUARTER, QUARTER), 0) == place).astype(jnp.float32)
        picked = jnp.dot(picks.T.astype(jnp.bfloat16), spectra, preferred_element_type=jnp.float32)
        for tile in range(3):
            for slot in range(2):
                rows_ref[pl.ds(tile * 2 + slot, N_BLK, stride=6), :] = picked[
                    slot * N_BLK : (slot + 1) * N_BLK, tile * 128 : (tile + 1) * 128
                ]
        own_rows = slice(q * N_BLK * 6, (q + 1) * N_BLK * 6)
        out_ref[own_rows, :] = rows_ref[...].astype(jnp.bfloat16)
        copies.append(pltpu.make_async_copy(out_ref.at[own_rows], out_hbm.at[own_rows], sems.at[q]))
        copies[-1].start()
    for copy in copies:
        copy.wait()


def own_part(core, own, window, table):
    hbm = pl.BlockSpec(memory_space=pltpu.HBM)
    vmem = pl.BlockSpec(memory_space=pltpu.VMEM)
    pinned = [pltpu.with_memory_space_constraint(x, pltpu.HBM) for x in (own, window, table)]
    half = pltpu.VMEM((128, HALF), jnp.bfloat16)
    return pl.pallas_call(
        own_kernel,
        in_specs=[pl.BlockSpec(memory_space=pltpu.SMEM), hbm, hbm, hbm],
        out_specs=[vmem] * 5,
        out_shape=[
            half,
            half,
            pltpu.VMEM((FRAME, 128), jnp.float32),
            pltpu.VMEM(window.shape, jnp.float32),
            pltpu.VMEM(table.shape, jnp.bfloat16),
        ],
        scratch_shapes=[pltpu.VMEM(own.shape, jnp.bfloat16), pltpu.SemaphoreType.DMA((3,))],
        compiler_params=pltpu.CompilerParams(vmem_limit_bytes=24 << 20),
        cost_estimate=pl.CostEstimate(flops=10_000_000, bytes_accessed=2_000_000, transcendentals=0),
        name="own",
    )(core, *pinned)


def channel_messages(core, own, other, lists):
    window = jnp.asarray(window_taps())
    table = jnp.asarray(fourier_halves())
    ua, va, frames, window, table = own_part(core, own, window, table)
    vmem = pl.BlockSpec(memory_space=pltpu.VMEM)
    return pl.pallas_call(
        channel_kernel,
        in_specs=[pl.BlockSpec(memory_space=pltpu.SMEM)] + [vmem] * 7,
        out_specs=pl.BlockSpec(memory_space=pltpu.HBM),
        out_shape=jax.ShapeDtypeStruct((N_FREQ * N_BLK * 6, 128), jnp.bfloat16),
        scratch_shapes=[
            pltpu.VMEM((256, HALF), jnp.bfloat16),
            pltpu.VMEM((256, HALF), jnp.bfloat16),
            pltpu.VMEM((N_BLK * 6, 128), jnp.float32),
            pltpu.VMEM((FRAME // 2, 128), jnp.float32),
            pltpu.VMEM((N_FREQ * N_BLK * 6, 128), jnp.bfloat16),
            pltpu.SemaphoreType.DMA((N_FREQ,)),
        ],
        compiler_params=pltpu.CompilerParams(vmem_limit_bytes=32 << 20),
        name="channels",
    )(core, frames, other, window, table, lists, ua, va)


def correlate_kernel(count_ref, got_ref, merge_ref, out_ref, rows_ref, right_all, even_all, odd_all, left_ref, right_ref):
    slot = pl.program_id(0)

    @pl.when(slot == 0)
    def _():
        sign = jnp.where(lax.broadcasted_iota(jnp.int32, (1, 128), 1) < 64, 1.0, -1.0)
        rows_ref[...] = got_ref[...].astype(jnp.float32)
        sources = {}
        for f in range(N_FREQ):
            for tile in range(3):
                start = f * N_BLK * 6 + tile * 2
                sources[f, tile] = jnp.concatenate(
                    [rows_ref[pl.ds(start + j, N_BLK, stride=6), :] for j in range(2)], axis=0
                ).astype(jnp.bfloat16)
        base = 0
        for pair, tiles in enumerate(GROUPS):
            depth = N_FREQ * len(tiles) * 128
            parts = [sources[f, tile] for f in range(N_FREQ) for tile in tiles]
            both = jnp.dot(
                jnp.concatenate(parts, axis=1),
                merge_ref[base : base + depth, :],
                preferred_element_type=jnp.float32,
            )
            base += depth
            for h in range(2):
                plain = both[:, h * 128 : (h + 1) * 128]
                turned = pltpu.roll(plain, 64, 1) * sign
                right_all[pl.ds(2 * pair + h, 256, stride=8), :] = plain
                left_all = (even_all, odd_all)[h]
                left_all[pl.ds(2 * pair, 256, stride=8), :] = plain
                left_all[pl.ds(2 * pair + 1, 256, stride=8), :] = turned

    live = slot < count_ref[0, 0]

    @pl.when(live)
    def _():
        def tile_of(ref, tile):
            return ref[pl.ds(pl.multiple_of(slot * 1024 + tile * 64, 64), 64), :].astype(jnp.bfloat16)

        for tile in range(TILES):
            rows = slice(tile * 64, tile * 64 + 64)
            left_ref[rows, :128] = tile_of(even_all, tile)
            left_ref[rows, 128:] = tile_of(odd_all, tile)
            right_ref[rows, :] = tile_of(right_all, tile)
        zero = jnp.zeros((64, 128), jnp.bfloat16)
        for m in range(TILES // 2):
            rhs = []
            for q in (2 * m, 2 * m + 1):
                column = right_ref[q * 64 : (q + 1) * 64, :]
                rhs.append(jnp.concatenate([column, zero], axis=1))
                rhs.append(jnp.concatenate([zero, column], axis=1))
            products = nt_dot(left_ref[: (2 * m + 2) * 64, :], jnp.concatenate(rhs, axis=0))
            for h in range(2):
                q = 2 * m + h
                for p in range(q + 1):
                    t = TILES * p - p * (p - 1) // 2 + q - p
                    piece = products[p * 64 : (p + 1) * 64, h * 128 : (h + 1) * 128]
                    out_ref[0, t] = (piece * (1.0 / 64.0)).astype(jnp.bfloat16)

    @pl.when(jnp.logical_not(live))
    def _():
        out_ref[...] = jnp.zeros(out_ref.shape, out_ref.dtype)


def visibility_tiles(counts, got):
    merge = jnp.asarray(merge_matrices())
    return pl.pallas_call(
        correlate_kernel,
        grid=(2,),
        in_specs=[
            pl.BlockSpec(memory_space=pltpu.SMEM),
            pl.BlockSpec((N_FREQ * N_BLK * 6, 128), lambda j: (0, 0)),
            pl.BlockSpec(merge.shape, lambda j: (0, 0)),
        ],
        out_specs=pl.BlockSpec((1, PAIRS, 64, 128), lambda j: (j, 0, 0, 0)),
        out_shape=jax.ShapeDtypeStruct((2, PAIRS, 64, 128), jnp.bfloat16),
        scratch_shapes=[
            pltpu.VMEM((N_FREQ * N_BLK * 6, 128), jnp.float32),
            pltpu.VMEM((2048, 128), jnp.float32),
            pltpu.VMEM((2048, 128), jnp.float32),
            pltpu.VMEM((2048, 128), jnp.float32),
            pltpu.VMEM((1024, 256), jnp.bfloat16),
            pltpu.VMEM((1024, 128), jnp.bfloat16),
        ],
        compiler_params=pltpu.CompilerParams(vmem_limit_bytes=40 << 20),
        name="correlate",
    )(counts, got, merge)


def shards(samples, channel_lists, channel_counts):
    core = lax.axis_index("core").astype(jnp.int32).reshape(1)
    other = lax.ppermute(samples, "core", [(0, 1), (1, 0)])
    lists = channel_lists.transpose(0, 2, 1)
    messages = channel_messages(core, samples, other, lists)
    got = lax.all_to_all(
        messages.reshape(N_FREQ * N_BLK, 3, 2, 128), ("z_hi", "core", "z_lo", "y", "x"), 0, 0, tiled=True
    ).reshape(N_FREQ * N_BLK * 6, 128)
    tiles = visibility_tiles(channel_counts, got)
    tiles = tiles.reshape(2, PAIRS, 32, 2, 128).transpose(0, 1, 3, 2, 4)
    return tiles.reshape(1, 1, 2, PAIRS, 2, 4096)


def solution(mesh):
    fine = Mesh(mesh.devices.reshape(8, 4, 4, 2, 2), ("z_lo", "y", "x", "z_hi", "core"))
    blk, freq = ("z_lo", "y", "x"), ("z_hi", "core")
    in_specs = (P(blk, freq, None), P(), P(freq, blk))
    out_specs = P(freq, blk, None, None, None, None)
    return jax.shard_map(shards, mesh=fine, in_specs=in_specs, out_specs=out_specs, check_vma=False)
```

```python
import math

import jax
import jax.numpy as jnp
import ml_dtypes
import numpy as np
from jax import lax
from jax.experimental import pallas as pl
from jax.experimental.pallas import tpu as pltpu
from jax.sharding import Mesh, PartitionSpec as P

FRAME = 2048
HALF = 1024
TAPS = 16
INS = 8
OUT_T = 24
QUARTER = 256
N_BLK = 128
N_FREQ = 4
TILES = 16
PAIRS = 136
GROUPS = ((0, 1), (0, 1), (1, 2), (1, 2))


def window_taps():
    total_len = FRAME * TAPS
    m = np.arange(total_len, dtype=np.float64)
    shaped = np.sinc((m - total_len / 2 + 0.5) / FRAME)
    shaped = shaped * (0.5 - 0.5 * np.cos(2.0 * np.pi * (m + 0.5) / total_len))
    shaped = shaped / np.sqrt(np.sum(shaped * shaped) / FRAME)
    return shaped.reshape(TAPS, FRAME).astype(np.float32)


def fourier_halves():
    channels = np.arange(1024).reshape(4, 128, 2).transpose(0, 2, 1)
    phase = channels[..., None] * np.arange(HALF) % FRAME
    angle = phase * (2.0 * np.pi / FRAME)
    scale = 1.0 / math.sqrt(FRAME)
    both = np.concatenate([np.cos(angle) * scale, -np.sin(angle) * scale], axis=2)
    return both.astype(np.float32).astype(ml_dtypes.bfloat16)


def message_lane(core, i, t, r):
    own = t - 8 * core
    if 0 <= own < 16:
        return i // 4 * 256 + 64 * r + own * 4 + i % 4
    return 128 + 64 * r + t % 8 * 8 + i


def merge_matrices():
    blocks = []
    for pair, tiles in enumerate(GROUPS):
        block = np.zeros((N_FREQ, len(tiles), 128, 2, 128), np.float32)
        for f in range(N_FREQ):
            for h in range(2):
                for t in range(OUT_T):
                    local = OUT_T * (f % 2) + t
                    if local > 46:
                        continue
                    spectrum = (32 * (f // 2) + local) % 64
                    for r in range(2):
                        lane = message_lane(f % 2, 2 * pair + h, t, r)
                        block[f, tiles.index(lane // 128), lane % 128, h, r * 64 + spectrum] = 1.0
        blocks.append(block.reshape(-1, 256))
    return np.concatenate(blocks).astype(ml_dtypes.bfloat16)


def nt_dot(a, b):
    return lax.dot_general(a, b, (((1,), (1,)), ((), ())), preferred_element_type=jnp.float32)


def spread(block_ref, first, frames, into_ref):
    for i in range(INS):
        for tile in range(FRAME // 128):
            values = block_ref[i, :, tile * 128 : (tile + 1) * 128].astype(jnp.float32)
            into_ref[pl.ds(tile * frames * 8 + i, frames, stride=8), :] = values[first : first + frames]


def by_fours(rows):
    first = lax.broadcasted_iota(jnp.int32, (8, 1), 0) < 4
    low = [jnp.where(first, a, pltpu.roll(b, 4, 0)) for a, b in zip(rows[::2], rows[1::2])]
    high = [jnp.where(first, pltpu.roll(a, 4, 0), b) for a, b in zip(rows[::2], rows[1::2])]
    return low + high


def fold_into(u_ref, v_ref, row, outputs, terms_of, frame_of, window_ref, order=list):
    def one(tile, carry):
        parts = []
        for half in (tile, tile + HALF // 128):
            lanes = pl.ds(pl.multiple_of(half * 128, 128), 128)
            taps = [jnp.broadcast_to(window_ref[k : k + 1, lanes], (8, 128)) for k in range(TAPS)]
            frames = {}
            totals = []
            for t in range(outputs):
                total = jnp.zeros((8, 128), jnp.float32)
                for k, m in terms_of(t):
                    if m not in frames:
                        frames[m] = frame_of(m, half)
                    total = total + taps[k] * frames[m]
                totals.append(total)
            parts.append(totals)
        lanes = pl.ds(pl.multiple_of(tile * 128, 128), 128)
        sums = order([low + high for low, high in zip(*parts)])
        differences = order([low - high for low, high in zip(*parts)])
        for t in range(0, outputs, 2):
            rows = slice(row + t * 8, row + t * 8 + 16)
            u_ref[rows, lanes] = jnp.concatenate(sums[t : t + 2], axis=0).astype(jnp.bfloat16)
            v_ref[rows, lanes] = jnp.concatenate(differences[t : t + 2], axis=0).astype(jnp.bfloat16)
        return carry

    lax.fori_loop(0, HALF // 128, one, 0, unroll=2)


def own_kernel(core_ref, own_hbm, window_hbm, table_hbm, u_ref, v_ref, frames_ref, window_ref, table_ref, own_ref, sems):
    copies = [
        pltpu.make_async_copy(own_hbm, own_ref, sems.at[0]),
        pltpu.make_async_copy(window_hbm, window_ref, sems.at[1]),
        pltpu.make_async_copy(table_hbm, table_ref, sems.at[2]),
    ]
    for copy in copies:
        copy.start()
    copies[0].wait()
    spread(own_ref, 0, 16, frames_ref)
    copies[1].wait()

    def frame_of(m, tile):
        return frames_ref[pl.ds(pl.multiple_of(tile * 128 + m * 8, 8), 8), :]

    second = core_ref[0] == 1

    @pl.when(jnp.logical_not(second))
    def _():
        fold_into(u_ref, v_ref, 0, 16, lambda t: [(15 - t + m, m) for m in range(t + 1)], frame_of, window_ref, by_fours)

    @pl.when(second)
    def _():
        fold_into(u_ref, v_ref, 0, 16, lambda t: [(m - t - 1, m) for m in range(t + 1, 16)], frame_of, window_ref, by_fours)

    copies[2].wait()


def channel_kernel(
    core_ref, frames_ref, other_ref, window_ref, table_ref, list_ref, ua_ref, va_ref, out_hbm, u_ref, v_ref, rows_ref, more_ref, out_ref, sems
):
    second = core_ref[0] == 1

    def own_frame(m, tile):
        return frames_ref[pl.ds(pl.multiple_of(tile * 128 + m * 8, 8), 8), :]

    def more_frame(m, tile):
        return more_ref[pl.ds(pl.multiple_of(tile * 64 + m * 8, 8), 8), :]

    def terms_of(t):
        return [(k, t + 1 + k) for k in range(TAPS)]

    @pl.when(jnp.logical_not(second))
    def _():
        spread(other_ref, 0, 8, more_ref)

        def frame_of(m, tile):
            return own_frame(m, tile) if m < 16 else more_frame(m - 16, tile)

        fold_into(u_ref, v_ref, 128, 8, terms_of, frame_of, window_ref)

    @pl.when(second)
    def _():
        spread(other_ref, 8, 8, more_ref)

        def frame_of(m, tile):
            return more_frame(m, tile) if m < 8 else own_frame(m - 8, tile)

        fold_into(u_ref, v_ref, 128, 8, terms_of, frame_of, window_ref)

    u_ref[:128, :] = ua_ref[...]
    v_ref[:128, :] = va_ref[...]
    u_ref[192:, :] = jnp.zeros((64, HALF), jnp.bfloat16)
    v_ref[192:, :] = jnp.zeros((64, HALF), jnp.bfloat16)

    low = lax.broadcasted_iota(jnp.int32, (1, 128), 1) < 64
    whole = [
        nt_dot(table_ref[:, parity].reshape(4 * 256, HALF), folded[...])
        for parity, folded in enumerate((u_ref, v_ref))
    ]
    copies = []
    for q in range(N_FREQ):
        halves = []
        for parity in range(2):
            y = whole[parity][q * 256 : (q + 1) * 256]
            re, im = y[:128, :128], y[128:, :128]
            rest = y[:128, 128:] + pltpu.roll(y[128:, 128:], 64, 1)
            first = jnp.where(low, re, pltpu.roll(im, 64, 1))
            last = jnp.where(low, pltpu.roll(re, 64, 1), im)
            halves.append(jnp.concatenate([first, rest, last], axis=1))
        spectra = jnp.concatenate(halves, axis=0).astype(jnp.bfloat16)
        channels = list_ref[q]
        place = (channels & 1) * 128 + ((channels & 255) >> 1)
        place = jnp.concatenate([place[:1], place[1:]], axis=1)
        picks = (lax.broadcasted_iota(jnp.int32, (QUARTER, QUARTER), 0) == place).astype(jnp.float32)
        picked = jnp.dot(picks.T.astype(jnp.bfloat16), spectra, preferred_element_type=jnp.float32)
        for tile in range(3):
            for slot in range(2):
                rows_ref[pl.ds(tile * 2 + slot, N_BLK, stride=6), :] = picked[
                    slot * N_BLK : (slot + 1) * N_BLK, tile * 128 : (tile + 1) * 128
                ]
        place_q = q % 2 * 2 + q // 2
        own_rows = slice(place_q * N_BLK * 6, (place_q + 1) * N_BLK * 6)
        out_ref[own_rows, :] = rows_ref[...].astype(jnp.bfloat16)
        copies.append(pltpu.make_async_copy(out_ref.at[own_rows], out_hbm.at[own_rows], sems.at[q]))
        copies[-1].start()
    for copy in copies:
        copy.wait()


def own_part(core, own, window, table):
    hbm = pl.BlockSpec(memory_space=pltpu.HBM)
    vmem = pl.BlockSpec(memory_space=pltpu.VMEM)
    pinned = [pltpu.with_memory_space_constraint(x, pltpu.HBM) for x in (own, window, table)]
    half = pltpu.VMEM((128, HALF), jnp.bfloat16)
    return pl.pallas_call(
        own_kernel,
        in_specs=[pl.BlockSpec(memory_space=pltpu.SMEM), hbm, hbm, hbm],
        out_specs=[vmem] * 5,
        out_shape=[
            half,
            half,
            pltpu.VMEM((FRAME, 128), jnp.float32),
            pltpu.VMEM(window.shape, jnp.float32),
            pltpu.VMEM(table.shape, jnp.bfloat16),
        ],
        scratch_shapes=[pltpu.VMEM(own.shape, jnp.bfloat16), pltpu.SemaphoreType.DMA((3,))],
        compiler_params=pltpu.CompilerParams(vmem_limit_bytes=24 << 20),
        cost_estimate=pl.CostEstimate(flops=10_000_000, bytes_accessed=2_000_000, transcendentals=0),
        name="own",
    )(core, *pinned)


def channel_messages(core, own, other, lists):
    window = jnp.asarray(window_taps())
    table = jnp.asarray(fourier_halves())
    ua, va, frames, window, table = own_part(core, own, window, table)
    vmem = pl.BlockSpec(memory_space=pltpu.VMEM)
    return pl.pallas_call(
        channel_kernel,
        in_specs=[pl.BlockSpec(memory_space=pltpu.SMEM)] + [vmem] * 7,
        out_specs=pl.BlockSpec(memory_space=pltpu.HBM),
        out_shape=jax.ShapeDtypeStruct((N_FREQ * N_BLK * 6, 128), jnp.bfloat16),
        scratch_shapes=[
            pltpu.VMEM((256, HALF), jnp.bfloat16),
            pltpu.VMEM((256, HALF), jnp.bfloat16),
            pltpu.VMEM((N_BLK * 6, 128), jnp.float32),
            pltpu.VMEM((FRAME // 2, 128), jnp.float32),
            pltpu.VMEM((N_FREQ * N_BLK * 6, 128), jnp.bfloat16),
            pltpu.SemaphoreType.DMA((N_FREQ,)),
        ],
        compiler_params=pltpu.CompilerParams(vmem_limit_bytes=32 << 20),
        name="channels",
    )(core, frames, other, window, table, lists, ua, va)


def correlate_kernel(count_ref, got_ref, merge_ref, out_ref, rows_ref, right_all, even_all, odd_all, left_ref, right_ref):
    slot = pl.program_id(0)

    @pl.when(slot == 0)
    def _():
        sign = jnp.where(lax.broadcasted_iota(jnp.int32, (1, 128), 1) < 64, 1.0, -1.0)
        rows_ref[...] = got_ref[...].astype(jnp.float32)
        sources = {}
        for f in range(N_FREQ):
            for tile in range(3):
                start = (f % 2 * 2 + f // 2) * N_BLK * 6 + tile * 2
                sources[f, tile] = jnp.concatenate(
                    [rows_ref[pl.ds(start + j, N_BLK, stride=6), :] for j in range(2)], axis=0
                ).astype(jnp.bfloat16)
        base = 0
        for pair, tiles in enumerate(GROUPS):
            depth = N_FREQ * len(tiles) * 128
            parts = [sources[f, tile] for f in range(N_FREQ) for tile in tiles]
            both = jnp.dot(
                jnp.concatenate(parts, axis=1),
                merge_ref[base : base + depth, :],
                preferred_element_type=jnp.float32,
            )
            base += depth
            for h in range(2):
                plain = both[:, h * 128 : (h + 1) * 128]
                turned = pltpu.roll(plain, 64, 1) * sign
                right_all[pl.ds(2 * pair + h, 256, stride=8), :] = plain
                left_all = (even_all, odd_all)[h]
                left_all[pl.ds(2 * pair, 256, stride=8), :] = plain
                left_all[pl.ds(2 * pair + 1, 256, stride=8), :] = turned

    live = slot < count_ref[0, 0]

    @pl.when(live)
    def _():
        def tile_of(ref, tile):
            return ref[pl.ds(pl.multiple_of(slot * 1024 + tile * 64, 64), 64), :].astype(jnp.bfloat16)

        for tile in range(TILES):
            rows = slice(tile * 64, tile * 64 + 64)
            left_ref[rows, :128] = tile_of(even_all, tile)
            left_ref[rows, 128:] = tile_of(odd_all, tile)
            right_ref[rows, :] = tile_of(right_all, tile)
        zero = jnp.zeros((64, 128), jnp.bfloat16)
        for m in range(TILES // 2):
            rhs = []
            for q in (2 * m, 2 * m + 1):
                column = right_ref[q * 64 : (q + 1) * 64, :]
                rhs.append(jnp.concatenate([column, zero], axis=1))
                rhs.append(jnp.concatenate([zero, column], axis=1))
            products = nt_dot(left_ref[: (2 * m + 2) * 64, :], jnp.concatenate(rhs, axis=0))
            for h in range(2):
                q = 2 * m + h
                for p in range(q + 1):
                    t = TILES * p - p * (p - 1) // 2 + q - p
                    piece = products[p * 64 : (p + 1) * 64, h * 128 : (h + 1) * 128]
                    out_ref[0, t] = (piece * (1.0 / 64.0)).astype(jnp.bfloat16)

    @pl.when(jnp.logical_not(live))
    def _():
        out_ref[...] = jnp.zeros(out_ref.shape, out_ref.dtype)


def visibility_tiles(counts, got):
    merge = jnp.asarray(merge_matrices())
    return pl.pallas_call(
        correlate_kernel,
        grid=(2,),
        in_specs=[
            pl.BlockSpec(memory_space=pltpu.SMEM),
            pl.BlockSpec((N_FREQ * N_BLK * 6, 128), lambda j: (0, 0)),
            pl.BlockSpec(merge.shape, lambda j: (0, 0)),
        ],
        out_specs=pl.BlockSpec((1, PAIRS, 64, 128), lambda j: (j, 0, 0, 0)),
        out_shape=jax.ShapeDtypeStruct((2, PAIRS, 64, 128), jnp.bfloat16),
        scratch_shapes=[
            pltpu.VMEM((N_FREQ * N_BLK * 6, 128), jnp.float32),
            pltpu.VMEM((2048, 128), jnp.float32),
            pltpu.VMEM((2048, 128), jnp.float32),
            pltpu.VMEM((2048, 128), jnp.float32),
            pltpu.VMEM((1024, 256), jnp.bfloat16),
            pltpu.VMEM((1024, 128), jnp.bfloat16),
        ],
        compiler_params=pltpu.CompilerParams(vmem_limit_bytes=40 << 20),
        name="correlate",
    )(counts, got, merge)


def shards(samples, channel_lists, channel_counts):
    core = lax.axis_index("core").astype(jnp.int32).reshape(1)
    other = lax.ppermute(samples, "core", [(0, 1), (1, 0)])
    lists = channel_lists.transpose(0, 2, 1)
    messages = channel_messages(core, samples, other, lists)
    got = lax.all_to_all(
        messages.reshape(N_FREQ * N_BLK, 3, 2, 128), ("core", "z_hi", "z_lo", "y", "x"), 0, 0, tiled=True
    ).reshape(N_FREQ * N_BLK * 6, 128)
    tiles = visibility_tiles(channel_counts, got)
    tiles = tiles.reshape(2, PAIRS, 32, 2, 128).transpose(0, 1, 3, 2, 4)
    return tiles.reshape(1, 1, 2, PAIRS, 2, 4096)


def solution(mesh):
    fine = Mesh(mesh.devices.reshape(8, 4, 4, 2, 2), ("z_lo", "y", "x", "z_hi", "core"))
    blk, freq = ("z_lo", "y", "x"), ("z_hi", "core")
    in_specs = (P(blk, freq, None), P(), P(freq, blk))
    out_specs = P(freq, blk, None, None, None, None)
    return jax.shard_map(shards, mesh=fine, in_specs=in_specs, out_specs=out_specs, check_vma=False)
```

```python
import math

import jax
import jax.numpy as jnp
import ml_dtypes
import numpy as np
from jax import lax
from jax.experimental import pallas as pl
from jax.experimental.pallas import tpu as pltpu
from jax.sharding import Mesh, PartitionSpec as P

FRAME = 2048
HALF = 1024
TAPS = 16
INS = 8
OUT_T = 24
QUARTER = 256
N_BLK = 128
N_FREQ = 4
TILES = 16
PAIRS = 136
GROUPS = ((0, 1), (0, 1), (1, 2), (1, 2))


def window_taps():
    total_len = FRAME * TAPS
    m = np.arange(total_len, dtype=np.float64)
    shaped = np.sinc((m - total_len / 2 + 0.5) / FRAME)
    shaped = shaped * (0.5 - 0.5 * np.cos(2.0 * np.pi * (m + 0.5) / total_len))
    shaped = shaped / np.sqrt(np.sum(shaped * shaped) / FRAME)
    return shaped.reshape(TAPS, FRAME).astype(np.float32)


def fourier_halves():
    channels = np.arange(1024).reshape(4, 128, 2).transpose(0, 2, 1)
    phase = channels[..., None] * np.arange(HALF) % FRAME
    angle = phase * (2.0 * np.pi / FRAME)
    scale = 1.0 / math.sqrt(FRAME)
    both = np.concatenate([np.cos(angle) * scale, -np.sin(angle) * scale], axis=2)
    return both.astype(np.float32).astype(ml_dtypes.bfloat16)


def message_lane(core, i, t, r):
    own = t - 8 * core
    if 0 <= own < 16:
        return i // 4 * 256 + 64 * r + own * 4 + i % 4
    return 128 + 64 * r + t % 8 * 8 + i


def merge_matrices():
    blocks = []
    for pair, tiles in enumerate(GROUPS):
        block = np.zeros((N_FREQ, len(tiles), 128, 2, 128), np.float32)
        for f in range(N_FREQ):
            for h in range(2):
                for t in range(OUT_T):
                    local = OUT_T * (f % 2) + t
                    if local > 46:
                        continue
                    spectrum = (32 * (f // 2) + local) % 64
                    for r in range(2):
                        lane = message_lane(f % 2, 2 * pair + h, t, r)
                        block[f, tiles.index(lane // 128), lane % 128, h, r * 64 + spectrum] = 1.0
        blocks.append(block.reshape(-1, 256))
    return np.concatenate(blocks).astype(ml_dtypes.bfloat16)


def nt_dot(a, b):
    return lax.dot_general(a, b, (((1,), (1,)), ((), ())), preferred_element_type=jnp.float32)


def spread(block_ref, first, frames, into_ref):
    for i in range(INS):
        for tile in range(FRAME // 128):
            values = block_ref[i, :, tile * 128 : (tile + 1) * 128].astype(jnp.float32)
            into_ref[pl.ds(tile * frames * 8 + i, frames, stride=8), :] = values[first : first + frames]


def by_fours(rows):
    first = lax.broadcasted_iota(jnp.int32, (8, 1), 0) < 4
    low = [jnp.where(first, a, pltpu.roll(b, 4, 0)) for a, b in zip(rows[::2], rows[1::2])]
    high = [jnp.where(first, pltpu.roll(a, 4, 0), b) for a, b in zip(rows[::2], rows[1::2])]
    return low + high


def fold_into(u_ref, v_ref, row, outputs, terms_of, frame_of, window_ref, order=list):
    def one(tile, carry):
        parts = []
        for half in (tile, tile + HALF // 128):
            lanes = pl.ds(pl.multiple_of(half * 128, 128), 128)
            taps = [jnp.broadcast_to(window_ref[k : k + 1, lanes], (8, 128)) for k in range(TAPS)]
            frames = {}
            totals = []
            for t in range(outputs):
                total = jnp.zeros((8, 128), jnp.float32)
                for k, m in terms_of(t):
                    if m not in frames:
                        frames[m] = frame_of(m, half)
                    total = total + taps[k] * frames[m]
                totals.append(total)
            parts.append(totals)
        lanes = pl.ds(pl.multiple_of(tile * 128, 128), 128)
        sums = order([low + high for low, high in zip(*parts)])
        differences = order([low - high for low, high in zip(*parts)])
        for t in range(0, outputs, 2):
            rows = slice(row + t * 8, row + t * 8 + 16)
            u_ref[rows, lanes] = jnp.concatenate(sums[t : t + 2], axis=0).astype(jnp.bfloat16)
            v_ref[rows, lanes] = jnp.concatenate(differences[t : t + 2], axis=0).astype(jnp.bfloat16)
        return carry

    lax.fori_loop(0, HALF // 128, one, 0, unroll=4)


def own_kernel(core_ref, own_hbm, window_hbm, table_hbm, u_ref, v_ref, frames_ref, window_ref, table_ref, own_ref, sems):
    copies = [
        pltpu.make_async_copy(own_hbm, own_ref, sems.at[0]),
        pltpu.make_async_copy(window_hbm, window_ref, sems.at[1]),
        pltpu.make_async_copy(table_hbm, table_ref, sems.at[2]),
    ]
    for copy in copies:
        copy.start()
    copies[0].wait()
    spread(own_ref, 0, 16, frames_ref)
    copies[1].wait()

    def frame_of(m, tile):
        return frames_ref[pl.ds(pl.multiple_of(tile * 128 + m * 8, 8), 8), :]

    second = core_ref[0] == 1

    @pl.when(jnp.logical_not(second))
    def _():
        fold_into(u_ref, v_ref, 0, 16, lambda t: [(15 - t + m, m) for m in range(t + 1)], frame_of, window_ref, by_fours)

    @pl.when(second)
    def _():
        fold_into(u_ref, v_ref, 0, 16, lambda t: [(m - t - 1, m) for m in range(t + 1, 16)], frame_of, window_ref, by_fours)

    copies[2].wait()


def channel_kernel(
    core_ref, frames_ref, other_ref, window_ref, table_ref, list_ref, ua_ref, va_ref, out_hbm, u_ref, v_ref, rows_ref, more_ref, out_ref, sems
):
    second = core_ref[0] == 1

    def own_frame(m, tile):
        return frames_ref[pl.ds(pl.multiple_of(tile * 128 + m * 8, 8), 8), :]

    def more_frame(m, tile):
        return more_ref[pl.ds(pl.multiple_of(tile * 64 + m * 8, 8), 8), :]

    def terms_of(t):
        return [(k, t + 1 + k) for k in range(TAPS)]

    @pl.when(jnp.logical_not(second))
    def _():
        spread(other_ref, 0, 8, more_ref)

        def frame_of(m, tile):
            return own_frame(m, tile) if m < 16 else more_frame(m - 16, tile)

        fold_into(u_ref, v_ref, 128, 8, terms_of, frame_of, window_ref)

    @pl.when(second)
    def _():
        spread(other_ref, 8, 8, more_ref)

        def frame_of(m, tile):
            return more_frame(m, tile) if m < 8 else own_frame(m - 8, tile)

        fold_into(u_ref, v_ref, 128, 8, terms_of, frame_of, window_ref)

    u_ref[:128, :] = ua_ref[...]
    v_ref[:128, :] = va_ref[...]
    u_ref[192:, :] = jnp.zeros((64, HALF), jnp.bfloat16)
    v_ref[192:, :] = jnp.zeros((64, HALF), jnp.bfloat16)

    low = lax.broadcasted_iota(jnp.int32, (1, 128), 1) < 64
    whole = [
        nt_dot(table_ref[:, parity].reshape(4 * 256, HALF), folded[...])
        for parity, folded in enumerate((u_ref, v_ref))
    ]
    copies = []
    for q in range(N_FREQ):
        halves = []
        for parity in range(2):
            y = whole[parity][q * 256 : (q + 1) * 256]
            re, im = y[:128, :128], y[128:, :128]
            rest = y[:128, 128:] + pltpu.roll(y[128:, 128:], 64, 1)
            first = jnp.where(low, re, pltpu.roll(im, 64, 1))
            last = jnp.where(low, pltpu.roll(re, 64, 1), im)
            halves.append(jnp.concatenate([first, rest, last], axis=1))
        spectra = jnp.concatenate(halves, axis=0).astype(jnp.bfloat16)
        channels = list_ref[q]
        place = (channels & 1) * 128 + ((channels & 255) >> 1)
        place = jnp.concatenate([place[:1], place[1:]], axis=1)
        picks = (lax.broadcasted_iota(jnp.int32, (QUARTER, QUARTER), 0) == place).astype(jnp.float32)
        picked = jnp.dot(picks.T.astype(jnp.bfloat16), spectra, preferred_element_type=jnp.float32)
        for tile in range(3):
            for slot in range(2):
                rows_ref[pl.ds(tile * 2 + slot, N_BLK, stride=6), :] = picked[
                    slot * N_BLK : (slot + 1) * N_BLK, tile * 128 : (tile + 1) * 128
                ]
        place_q = q % 2 * 2 + q // 2
        own_rows = slice(place_q * N_BLK * 6, (place_q + 1) * N_BLK * 6)
        out_ref[own_rows, :] = rows_ref[...].astype(jnp.bfloat16)
        copies.append(pltpu.make_async_copy(out_ref.at[own_rows], out_hbm.at[own_rows], sems.at[q]))
        copies[-1].start()
    for copy in copies:
        copy.wait()


def own_part(core, own, window, table):
    hbm = pl.BlockSpec(memory_space=pltpu.HBM)
    vmem = pl.BlockSpec(memory_space=pltpu.VMEM)
    pinned = [pltpu.with_memory_space_constraint(x, pltpu.HBM) for x in (own, window, table)]
    half = pltpu.VMEM((128, HALF), jnp.bfloat16)
    return pl.pallas_call(
        own_kernel,
        in_specs=[pl.BlockSpec(memory_space=pltpu.SMEM), hbm, hbm, hbm],
        out_specs=[vmem] * 5,
        out_shape=[
            half,
            half,
            pltpu.VMEM((FRAME, 128), jnp.float32),
            pltpu.VMEM(window.shape, jnp.float32),
            pltpu.VMEM(table.shape, jnp.bfloat16),
        ],
        scratch_shapes=[pltpu.VMEM(own.shape, jnp.bfloat16), pltpu.SemaphoreType.DMA((3,))],
        compiler_params=pltpu.CompilerParams(vmem_limit_bytes=24 << 20),
        cost_estimate=pl.CostEstimate(flops=10_000_000, bytes_accessed=2_000_000, transcendentals=0),
        name="own",
    )(core, *pinned)


def channel_messages(core, own, other, lists):
    window = jnp.asarray(window_taps())
    table = jnp.asarray(fourier_halves())
    ua, va, frames, window, table = own_part(core, own, window, table)
    vmem = pl.BlockSpec(memory_space=pltpu.VMEM)
    return pl.pallas_call(
        channel_kernel,
        in_specs=[pl.BlockSpec(memory_space=pltpu.SMEM)] + [vmem] * 7,
        out_specs=pl.BlockSpec(memory_space=pltpu.HBM),
        out_shape=jax.ShapeDtypeStruct((N_FREQ * N_BLK * 6, 128), jnp.bfloat16),
        scratch_shapes=[
            pltpu.VMEM((256, HALF), jnp.bfloat16),
            pltpu.VMEM((256, HALF), jnp.bfloat16),
            pltpu.VMEM((N_BLK * 6, 128), jnp.float32),
            pltpu.VMEM((FRAME // 2, 128), jnp.float32),
            pltpu.VMEM((N_FREQ * N_BLK * 6, 128), jnp.bfloat16),
            pltpu.SemaphoreType.DMA((N_FREQ,)),
        ],
        compiler_params=pltpu.CompilerParams(vmem_limit_bytes=32 << 20),
        name="channels",
    )(core, frames, other, window, table, lists, ua, va)


def correlate_kernel(count_ref, got_ref, merge_ref, out_ref, rows_ref, right_all, even_all, odd_all, left_ref, right_ref):
    slot = pl.program_id(0)

    @pl.when(slot == 0)
    def _():
        sign = jnp.where(lax.broadcasted_iota(jnp.int32, (1, 128), 1) < 64, 1.0, -1.0)
        rows_ref[...] = got_ref[...].astype(jnp.float32)
        sources = {}
        for f in range(N_FREQ):
            for tile in range(3):
                start = (f % 2 * 2 + f // 2) * N_BLK * 6 + tile * 2
                sources[f, tile] = jnp.concatenate(
                    [rows_ref[pl.ds(start + j, N_BLK, stride=6), :] for j in range(2)], axis=0
                ).astype(jnp.bfloat16)
        base = 0
        for pair, tiles in enumerate(GROUPS):
            depth = N_FREQ * len(tiles) * 128
            parts = [sources[f, tile] for f in range(N_FREQ) for tile in tiles]
            both = jnp.dot(
                jnp.concatenate(parts, axis=1),
                merge_ref[base : base + depth, :],
                preferred_element_type=jnp.float32,
            )
            base += depth
            for h in range(2):
                plain = both[:, h * 128 : (h + 1) * 128]
                turned = pltpu.roll(plain, 64, 1) * sign
                right_all[pl.ds(2 * pair + h, 256, stride=8), :] = plain
                left_all = (even_all, odd_all)[h]
                left_all[pl.ds(2 * pair, 256, stride=8), :] = plain
                left_all[pl.ds(2 * pair + 1, 256, stride=8), :] = turned

    live = slot < count_ref[0, 0]

    @pl.when(live)
    def _():
        def tile_of(ref, tile):
            return ref[pl.ds(pl.multiple_of(slot * 1024 + tile * 64, 64), 64), :].astype(jnp.bfloat16)

        for tile in range(TILES):
            rows = slice(tile * 64, tile * 64 + 64)
            left_ref[rows, :128] = tile_of(even_all, tile)
            left_ref[rows, 128:] = tile_of(odd_all, tile)
            right_ref[rows, :] = tile_of(right_all, tile)
        zero = jnp.zeros((64, 128), jnp.bfloat16)
        for m in range(TILES // 2):
            rhs = []
            for q in (2 * m, 2 * m + 1):
                column = right_ref[q * 64 : (q + 1) * 64, :]
                rhs.append(jnp.concatenate([column, zero], axis=1))
                rhs.append(jnp.concatenate([zero, column], axis=1))
            products = nt_dot(left_ref[: (2 * m + 2) * 64, :], jnp.concatenate(rhs, axis=0))
            for h in range(2):
                q = 2 * m + h
                for p in range(q + 1):
                    t = TILES * p - p * (p - 1) // 2 + q - p
                    piece = products[p * 64 : (p + 1) * 64, h * 128 : (h + 1) * 128]
                    out_ref[0, t] = (piece * (1.0 / 64.0)).astype(jnp.bfloat16)

    @pl.when(jnp.logical_not(live))
    def _():
        out_ref[...] = jnp.zeros(out_ref.shape, out_ref.dtype)


def visibility_tiles(counts, got):
    merge = jnp.asarray(merge_matrices())
    return pl.pallas_call(
        correlate_kernel,
        grid=(2,),
        in_specs=[
            pl.BlockSpec(memory_space=pltpu.SMEM),
            pl.BlockSpec((N_FREQ * N_BLK * 6, 128), lambda j: (0, 0)),
            pl.BlockSpec(merge.shape, lambda j: (0, 0)),
        ],
        out_specs=pl.BlockSpec((1, PAIRS, 64, 128), lambda j: (j, 0, 0, 0)),
        out_shape=jax.ShapeDtypeStruct((2, PAIRS, 64, 128), jnp.bfloat16),
        scratch_shapes=[
            pltpu.VMEM((N_FREQ * N_BLK * 6, 128), jnp.float32),
            pltpu.VMEM((2048, 128), jnp.float32),
            pltpu.VMEM((2048, 128), jnp.float32),
            pltpu.VMEM((2048, 128), jnp.float32),
            pltpu.VMEM((1024, 256), jnp.bfloat16),
            pltpu.VMEM((1024, 128), jnp.bfloat16),
        ],
        compiler_params=pltpu.CompilerParams(vmem_limit_bytes=40 << 20),
        name="correlate",
    )(counts, got, merge)


def shards(samples, channel_lists, channel_counts):
    core = lax.axis_index("core").astype(jnp.int32).reshape(1)
    other = lax.ppermute(samples, "core", [(0, 1), (1, 0)])
    lists = channel_lists.transpose(0, 2, 1)
    messages = channel_messages(core, samples, other, lists)
    got = lax.all_to_all(
        messages.reshape(N_FREQ * N_BLK, 3, 2, 128), ("core", "z_hi", "z_lo", "y", "x"), 0, 0, tiled=True
    ).reshape(N_FREQ * N_BLK * 6, 128)
    tiles = visibility_tiles(channel_counts, got)
    tiles = tiles.reshape(2, PAIRS, 32, 2, 128).transpose(0, 1, 3, 2, 4)
    return tiles.reshape(1, 1, 2, PAIRS, 2, 4096)


def solution(mesh):
    fine = Mesh(mesh.devices.reshape(8, 4, 4, 2, 2), ("z_lo", "y", "x", "z_hi", "core"))
    blk, freq = ("z_lo", "y", "x"), ("z_hi", "core")
    in_specs = (P(blk, freq, None), P(), P(freq, blk))
    out_specs = P(freq, blk, None, None, None, None)
    return jax.shard_map(shards, mesh=fine, in_specs=in_specs, out_specs=out_specs, check_vma=False)
```
